128 devices in a mesh: dp: 4 (over x), shard: 32 (over z, y, core).
Axes of the slice: x: 4, y: 4, z: 4, core: 2. Of those that a mesh axis runs over, the one named last changes fastest.
Arguments:
- tokens: bfloat16 [65536, 1024], P(('dp', 'shard')), may hold values from -6 to 6
- cotangent: bfloat16 [65536, 1024], P(('dp', 'shard')), may hold values from -6 to 6
- lengths: int32 [128, 4], P(('dp', 'shard')), may hold values from 1 to 256, 512 in all within a row
- levels: int32 [128, 4], P(('dp', 'shard')), may hold values from 0 to 7
- level_scale: float32 [8], replicated, may hold values from 0.25 to 4
- norm_gain: float32 [1024], replicated, may hold values from 0.25 to 1.75
- q_gain: float32 [128], replicated, may hold values from 0.5 to 3
- k_gain: float32 [128], replicated, may hold values from 0.5 to 3
- w_query: bfloat16 [1024, 2048], P('shard'), may hold values from -0.1875 to 0.1875
- w_key: bfloat16 [1024, 1024], P('shard'), may hold values from -0.1875 to 0.1875
- w_value: bfloat16 [1024, 1024], P('shard'), may hold values from -0.1875 to 0.1875
- w_output: bfloat16 [2048, 1024], P('shard'), may hold values from -0.125 to 0.125
Outputs:
- grad_tokens: bfloat16 [65536, 1024], P(('dp', 'shard'))
- grad_norm_gain: float32 [1024], replicated
- grad_q_gain: float32 [128], replicated
- grad_k_gain: float32 [128], replicated
- grad_w_query: float32 [1024, 2048], P('shard')
- grad_w_key: float32 [1024, 1024], P('shard')
- grad_w_value: float32 [1024, 1024], P('shard')
- grad_w_output: float32 [2048, 1024], P('shard')
The draws below stay inside these ranges and needn't reach their ends.
Inputs may be any that keep to these rules, and one draw needn't show every extreme that they name: `lengths`: each row's 4 entries sum to 512; the last entry of a row counts padding tokens; every row has an entry equal to 256.
All inputs are finite; a program needn't handle non-finite values.
Results may differ from the reference program's by a relative error of at most 0.03.
Values may be sent and summed in bfloat16 or wider, within the bound.
No kernel may reach another device: no remote copies, remote signals or barrier semaphores. Data moves between devices by JAX's collectives and lax.ppermute only.
A program may use at most 128 MiB of HBM per device.

```python
import math
import jax
import jax.numpy as jnp
import numpy as np
from jax import lax

D = 1024
HD = 128
TOK_DEV = 512
DOCS = 4
LEVELS = 8
MOST = 256
QD = 2048
KD = 1024
ROWS = 128
TOKENS = 65536


def head_gains(key, lower, upper):
    return jax.random.uniform(key, (HD,), jnp.float32, lower, upper)


def draw_q_gain(key, part):
    key = jax.random.fold_in(key, 11)
    return head_gains(key, 0.5, 1.6)


def draw_k_gain(key, part):
    key = jax.random.fold_in(key, 23)
    return head_gains(key, 0.5, 1.6)


def with_ends(result, rng, smallest, largest):
    shape = result.shape
    index_at = [jax.random.randint(jax.random.fold_in(rng, axis), (), 0, shape[axis]) for axis in range(len(shape))]
    result = result.at[tuple(index_at)].set(smallest)
    longest = shape.index(max(shape))
    index_at[longest] = (index_at[longest] + 1) % shape[longest]
    return result.at[tuple(index_at)].set(largest)


def shard_levels(own_key, dims, shards, smallest, high):
    level = 1.0
    for dim, blocks in shards:
        steps = jax.random.uniform(jax.random.fold_in(jax.random.fold_in(own_key, 6), dim), (blocks,), jnp.float32, smallest / len(shards), high / len(shards))
        level = level * jnp.repeat(jnp.exp(steps), dims[dim] // blocks).reshape((-1,) + (1,) * (len(dims) - 1 - dim))
    return level


def split_up(amount, total, most, slope):
    loads = [(1 << 20) // math.isqrt(standing ** slope) + 1 for standing in range(2, amount + 1)]
    spare, holding = total - most - (amount - 1), [1] * (amount - 1)
    while spare > 0:
        candidates = [i for i in range(amount - 1) if holding[i] < most]
        pool, budget = sum([loads[i] for i in candidates]), spare
        for i in candidates:
            more = min(most - holding[i], max(1, budget * loads[i] // pool), spare)
            holding[i] = holding[i] + more
            spare = spare - more
    return np.array([most] + holding)


def uneven(rng, count, total, most, slope):
    if count == 2:
        one = jax.random.randint(rng, (), max(1, total - most), min(most, total - 1) + 1)
        return jnp.stack([one, total - one])
    tallies = jnp.asarray(split_up(count, total, most, slope), jnp.int32)
    pairs = (count - 1) // 2
    source_of, sink = tallies[1:1 + 2 * pairs:2], tallies[2:2 + 2 * pairs:2]
    room = jnp.minimum(source_of - 1, most - sink)
    moved = jax.random.randint(jax.random.fold_in(rng, 1), (pairs,), 0, 1 << 20) % (room + 1)
    tallies = tallies.at[1:1 + 2 * pairs:2].set(source_of - moved).at[2:2 + 2 * pairs:2].set(sink + moved)
    return tallies[jax.random.permutation(jax.random.fold_in(rng, 2), count)]


def bell_draw(rng, dims, scale, most, cuts=(), kind=jnp.bfloat16):
    gain = shard_levels(rng, dims, cuts, -0.22, 0.18) if cuts else 1.0
    entries = jax.random.normal(rng, dims, jnp.float32) * scale * gain
    return jnp.minimum(jnp.maximum(entries, -most), most).astype(kind)


def setup_inputs(seed: int = 0) -> dict:
    key_list = jax.random.split(jax.random.key(seed), 13)
    return {
        "tokens": bell_draw(key_list[0], (TOKENS, D), 1.0, 6.0, ((0, 128),)),
        "cotangent": bell_draw(key_list[1], (TOKENS, D), 1.0, 6.0, ((0, 128),)),
        "lengths": jax.vmap(lambda own: uneven(own, DOCS, TOK_DEV, MOST, 2))(jax.random.split(key_list[2], ROWS)).reshape((ROWS, DOCS)).astype(jnp.int32),
        "levels": with_ends(jax.random.randint(key_list[3], (ROWS, DOCS), 0, LEVELS), jax.random.fold_in(key_list[3], 1), 0, LEVELS - 1).astype(jnp.int32),
        "level_scale": jnp.clip(jnp.exp(jax.random.uniform(key_list[4], (LEVELS,), jnp.float32, math.log(0.25), math.log(4.0))), 0.25, 4.0),
        "norm_gain": jnp.clip(1.0 + 0.15 * jax.random.normal(key_list[5], (D,), jnp.float32), 0.25, 1.75),
        "q_gain": draw_q_gain(jax.random.fold_in(key_list[12], 71), 0),
        "k_gain": draw_k_gain(jax.random.fold_in(key_list[12], 71), 0),
        "w_query": bell_draw(key_list[8], (D, QD), D ** -0.5, 0.1875, ((0, 32),)),
        "w_key": bell_draw(key_list[9], (D, KD), D ** -0.5, 0.1875, ((0, 32),)),
        "w_value": bell_draw(key_list[10], (D, KD), D ** -0.5, 0.1875, ((0, 32),)),
        "w_output": bell_draw(key_list[11], (QD, D), QD ** -0.5, 0.125, ((0, 32),)),
    }


norm_eps = 1e-06
rope_theta = 1000000.0

def row_layout(lengths, levels, level_scale, rows_total):
    slot_ends = jnp.cumsum(lengths).astype(jnp.int32)
    slot_starts = (slot_ends - lengths).astype(jnp.int32)
    places = jnp.arange(rows_total, dtype=jnp.int32)
    owner = lax.optimization_barrier(jnp.sum((places[:, None] >= slot_ends[None, :]).astype(jnp.int32), axis=1)).astype(jnp.int32)
    slot_ids = jnp.arange(lengths.shape[0], dtype=jnp.int32)
    member = owner[:, None] == slot_ids[None, :]
    positions = places - lax.optimization_barrier(jnp.sum(jnp.where(member, slot_starts[None, :], 0), axis=1)).astype(jnp.int32)
    level_ids = jnp.arange(level_scale.shape[0], dtype=jnp.int32)
    level_hit = levels[:, None] == level_ids[None, :]
    slot_weight = lax.optimization_barrier(jnp.sum(jnp.where(level_hit, level_scale[None, :], jnp.float32(0.0)), axis=1))
    slot_weight = jnp.where(slot_ids < lengths.shape[0] - 1, slot_weight, jnp.float32(0.0))
    token_weight = lax.optimization_barrier(jnp.sum(jnp.where(member, slot_weight[None, :], jnp.float32(0.0)), axis=1))
    return (owner, positions, token_weight)

def head_norm(heads_in, gains):
    factor = lax.rsqrt(lax.optimization_barrier(jnp.mean(heads_in * heads_in, axis=-1, keepdims=True)) + norm_eps)
    return heads_in * factor * gains

def rotate(heads_in, positions):
    head_dim = heads_in.shape[-1]
    half_dim = head_dim // 2
    freqs = rope_theta ** (-jnp.arange(half_dim, dtype=jnp.float32) * 2.0 / head_dim)
    angles = positions.astype(jnp.float32)[:, None] * freqs[None, :]
    cosine = jnp.cos(angles)
    sines = jnp.sin(angles)
    cosine = jnp.concatenate([cosine, cosine], axis=-1)[:, None, :]
    sines = jnp.concatenate([sines, sines], axis=-1)[:, None, :]
    turned = jnp.concatenate([-heads_in[..., half_dim:], heads_in[..., :half_dim]], axis=-1)
    return heads_in * cosine + turned * sines

def layer_branch(tokens_in, norm_gain, q_gain, k_gain, w_query, w_key, w_value, w_output, owner, positions):
    rows_total = tokens_in.shape[0]
    head_dim = q_gain.shape[0]
    query_heads = w_query.shape[1] // head_dim
    key_heads = w_key.shape[1] // head_dim
    group_size = query_heads // key_heads
    widened = tokens_in.astype(jnp.float32)
    inverse = lax.rsqrt(lax.optimization_barrier(jnp.mean(widened * widened, axis=-1, keepdims=True)) + norm_eps)
    normed = (widened * inverse * norm_gain).astype(jnp.bfloat16)
    queries = jnp.dot(normed, w_query, preferred_element_type=jnp.float32).reshape(rows_total, query_heads, head_dim)
    keys_all = jnp.dot(normed, w_key, preferred_element_type=jnp.float32).reshape(rows_total, key_heads, head_dim)
    values_all = jnp.dot(normed, w_value, preferred_element_type=jnp.float32).astype(jnp.bfloat16)
    values_all = values_all.reshape(rows_total, key_heads, head_dim)
    queries = rotate(head_norm(queries, q_gain), positions).astype(jnp.bfloat16)
    keys_all = rotate(head_norm(keys_all, k_gain), positions).astype(jnp.bfloat16)
    grouped = queries.reshape(rows_total, key_heads, group_size, head_dim)
    scores = jnp.einsum('tkgd,skd->kgts', grouped.astype(jnp.float32), keys_all.astype(jnp.float32))
    scores = scores * (1.0 / math.sqrt(head_dim))
    places = jnp.arange(rows_total, dtype=jnp.int32)
    allowed = (owner[:, None] == owner[None, :]) & (places[None, :] <= places[:, None])
    scores = jnp.where(allowed, scores, jnp.float32(-1e+30))
    highest = lax.stop_gradient(lax.optimization_barrier(jnp.max(scores, axis=-1, keepdims=True)))
    raised = jnp.exp(scores - highest)
    probs = (raised / lax.optimization_barrier(jnp.sum(raised, axis=-1, keepdims=True))).astype(jnp.bfloat16)
    mixed = jnp.einsum('kgts,skd->tkgd', probs.astype(jnp.float32), values_all.astype(jnp.float32))
    mixed = mixed.astype(jnp.bfloat16).reshape(rows_total, query_heads * head_dim)
    return widened + jnp.dot(mixed, w_output, preferred_element_type=jnp.float32)

def row_grads(tokens_row, cotangent_row, length_row, level_row, level_scale, norm_gain, q_gain, k_gain, w_query, w_key, w_value, w_output):
    owner, positions, token_weight = row_layout(length_row, level_row, level_scale, tokens_row.shape[0])

    def branch(tokens_in, gain_in, gain_query, gain_key, proj_query, proj_key, proj_value, proj_output):
        return layer_branch(tokens_in, gain_in, gain_query, gain_key, proj_query, proj_key, proj_value, proj_output, owner, positions)
    _, pullback = jax.vjp(branch, tokens_row, norm_gain, q_gain, k_gain, w_query, w_key, w_value, w_output)
    return pullback(cotangent_row.astype(jnp.float32) * token_weight[:, None])

def reference(tokens, cotangent, lengths, levels, level_scale, norm_gain, q_gain, k_gain, w_query, w_key, w_value, w_output):
    token_rows = tokens.reshape(ROWS, TOK_DEV, D)
    cotangent_rows = cotangent.reshape(ROWS, TOK_DEV, D)
    params = (norm_gain, q_gain, k_gain, w_query, w_key, w_value, w_output)

    def visit(running, inputs):
        tokens_row, cotangent_row, length_row, level_row = inputs
        gradients = row_grads(tokens_row, cotangent_row, length_row, level_row, level_scale, *params)
        updated = tuple((summed + gradient.astype(jnp.float32) for summed, gradient in zip(running, gradients[1:])))
        return (updated, gradients[0])
    start = tuple((jnp.zeros(operand.shape, jnp.float32) for operand in params))
    totals, input_grads = lax.scan(visit, start, (token_rows, cotangent_rows, lengths, levels))
    factor = 1.0 / math.sqrt(TOKENS)
    return (input_grads.reshape(TOKENS, D), totals[0] * factor, totals[1] * factor, totals[2] * factor, totals[3] * factor, totals[4] * factor, totals[5] * factor, totals[6] * factor)
```

```python
import functools
import math

import jax
import jax.numpy as jnp
from jax import lax
from jax.experimental import pallas as pl
from jax.experimental.pallas import tpu as pltpu
from jax.sharding import Mesh
from jax.sharding import PartitionSpec as P

norm_eps = 1e-06
rope_theta = 1000000.0
HD = 128
T = 512
D = 1024
HALF = T // 2
NEG = -1e30
LOG2E = 1.4426950408889634
SCALE = 1.0 / math.sqrt(HD)
ALL = ("dp", "z", "y", "core")
VMEM_LIMIT = 56 * 1024 * 1024
BF = jnp.bfloat16
F32 = jnp.float32


def params(**kw):
    return pltpu.CompilerParams(vmem_limit_bytes=VMEM_LIMIT, **kw)


def shift(x, axis, by):
    n = lax.axis_size(axis)
    return lax.ppermute(x, axis, [(i, (i + by) % n) for i in range(n)])


def swap(x):
    return lax.ppermute(x, "core", [(0, 1), (1, 0)])


def dot_nt(a, b):
    return lax.dot_general(a, b, (((1,), (1,)), ((), ())), preferred_element_type=F32)


def dot_tn(a, b):
    return lax.dot_general(a, b, (((0,), (0,)), ((), ())), preferred_element_type=F32)


def row_layout(lengths, levels, level_scale):
    ends = jnp.cumsum(lengths, axis=1)
    starts = ends - lengths
    places = jnp.arange(T, dtype=jnp.int32)
    owner = jnp.sum((places[None, :, None] >= ends[:, None, :]).astype(jnp.int32), axis=2)
    slots = jnp.arange(lengths.shape[1], dtype=jnp.int32)
    member = owner[:, :, None] == slots[None, None, :]
    positions = places[None, :] - jnp.sum(jnp.where(member, starts[:, None, :], 0), axis=2)
    hit = levels[:, :, None] == jnp.arange(level_scale.shape[0], dtype=jnp.int32)[None, None, :]
    slot_weight = jnp.sum(jnp.where(hit, level_scale[None, None, :], F32(0.0)), axis=2)
    slot_weight = jnp.where(slots[None, :] < lengths.shape[1] - 1, slot_weight, F32(0.0))
    weight = jnp.sum(jnp.where(member, slot_weight[:, None, :], F32(0.0)), axis=2)
    return owner, positions, weight


def gather_line(x, axis):
    half = x.shape[0] // 2
    nxt, prv = shift(x, axis, -1), shift(x, axis, 1)
    far_a, far_b = shift(nxt[:half], axis, -1), shift(prv[half:], axis, 1)
    return x, nxt, far_a, far_b, prv


def gather_small(x, axis):
    return jnp.concatenate([x, shift(x, axis, -1), shift(x, axis, 2), shift(x, axis, 1)], 0)


def project_kernel(ids, normed, cos, sin, qg, kg, *refs):
    a_refs, b_refs = refs[:5], refs[5:10]
    q_out, k_out, v_out, uq_out, uk_out, wq, wkv = refs[10:]
    z, y = ids[0], ids[1]

    @pl.when(pl.program_id(0) == 0)
    def _():
        def block(group, r, s):
            if r == 2:
                ref = group[2] if s < 2 else group[3]
                return ref[pl.ds(64 * (s % 2), 64), :]
            return group[r if r < 2 else 4][pl.ds(64 * s, 64), :]

        for r in range(4):
            for s in range(4):
                za, ya = lax.rem(z + r, 4), lax.rem(y + s, 4)
                wq[pl.ds(pl.multiple_of(za * 256 + ya * 64, 64), 64), :] = block(a_refs, r, s)
                zb, yb = lax.rem(z + s, 4), lax.rem(y + r, 4)
                wkv[pl.ds(pl.multiple_of(zb * 256 + yb * 64, 64), 64), :] = block(b_refs, r, s)

    x = normed[...]
    c, s = cos[...], sin[...]

    def turn(u, gain):
        n = u * lax.rsqrt(jnp.mean(u * u, axis=-1, keepdims=True) + norm_eps) * gain
        return n * c + pltpu.roll(n, 64, 1) * s

    kv = jnp.dot(x, wkv[...], preferred_element_type=F32)
    v_out[...] = kv[:, 512:].astype(BF)
    uk_out[...] = kv[:, :512]
    for h in range(4):
        cols = slice(h * HD, (h + 1) * HD)
        k_out[:, cols] = turn(kv[:, cols], kg[...]).astype(BF)
    q = jnp.dot(x, wq[...], preferred_element_type=F32)
    uq_out[...] = q
    for h in range(8):
        cols = slice(h * HD, (h + 1) * HD)
        q_out[:, cols] = turn(q[:, cols], qg[...]).astype(BF)


def project(ids, normed, cos, sin, qg, kg, a_parts, b_parts):
    rows = normed.shape[0]
    step = 256

    def by_row(cols):
        return pl.BlockSpec((step, cols), lambda i: (i, 0))

    def whole(x):
        return pl.BlockSpec(x.shape, lambda i: (0,) * x.ndim)

    wide = jax.ShapeDtypeStruct((D, D), BF)
    return pl.pallas_call(
        project_kernel,
        grid=(rows // step,),
        in_specs=[pl.BlockSpec(memory_space=pltpu.SMEM), by_row(D), by_row(HD), by_row(HD), whole(qg), whole(kg)]
        + [whole(x) for x in a_parts + b_parts],
        out_specs=[by_row(1024), by_row(512), by_row(512), by_row(1024), by_row(512), whole(wide), whole(wide)],
        out_shape=[
            jax.ShapeDtypeStruct((rows, 1024), BF),
            jax.ShapeDtypeStruct((rows, 512), BF),
            jax.ShapeDtypeStruct((rows, 512), BF),
            jax.ShapeDtypeStruct((rows, 1024), F32),
            jax.ShapeDtypeStruct((rows, 512), F32),
            wide,
            wide,
        ],
        compiler_params=params(),
        cost_estimate=pl.CostEstimate(flops=2 * rows * D * 2048, bytes_accessed=20 << 20, transcendentals=0),
        name="project",
    )(ids, normed, cos, sin, qg, kg, *a_parts, *b_parts)


def fill_bias(own_col, own_lane, bias):
    s = lax.broadcasted_iota(jnp.int32, (T, T), 0)
    t = lax.broadcasted_iota(jnp.int32, (T, T), 1)
    allowed = (own_col[0] == own_lane[0]) & (s <= t)
    bias[...] = jnp.where(allowed, F32(0.0), F32(NEG))


TILES = ((0, HALF, HALF), (HALF, T, T))


def forward_kernel(ids, q, k, v, own_col, own_lane, keep, send, lse, bias):
    @pl.when(pl.program_id(1) == 0)
    def _():
        fill_bias(own_col, own_lane, bias)

    parts = []
    for h in range(2):
        tiles = []
        for lo, hi, keys in TILES:
            qh = q[lo:hi, h * HD : (h + 1) * HD]
            s = dot_nt(k[:keys, :], qh) * F32(SCALE * LOG2E) + bias[:keys, lo:hi]
            top = jnp.max(s, axis=0, keepdims=True)
            p = jnp.exp2(s - top)
            total = jnp.sum(p, axis=0, keepdims=True)
            lse[0, h : h + 1, lo:hi] = top + jnp.log2(total)
            p = (p * (1.0 / total)).astype(BF)
            tiles.append(dot_tn(v[:keys, :], p))
        parts.append(jnp.concatenate(tiles, axis=1))
    low = jnp.concatenate([parts[0][:64], parts[1][:64]], axis=0).T.astype(BF)
    high = jnp.concatenate([parts[0][64:], parts[1][64:]], axis=0).T.astype(BF)

    @pl.when(ids[2] == 0)
    def _():
        keep[...] = low
        send[...] = high

    @pl.when(ids[2] == 1)
    def _():
        keep[...] = high
        send[...] = low


def attend(ids, q, k, v, own_col, own_lane):
    rows = q.shape[0] // T
    heads = k.shape[1] // HD
    half = jax.ShapeDtypeStruct((rows * T, heads * HD), BF)
    return pl.pallas_call(
        forward_kernel,
        grid=(rows, heads),
        in_specs=[
            pl.BlockSpec(memory_space=pltpu.SMEM),
            pl.BlockSpec((T, 2 * HD), lambda r, h: (r, h)),
            pl.BlockSpec((T, HD), lambda r, h: (r, h)),
            pl.BlockSpec((T, HD), lambda r, h: (r, h)),
            pl.BlockSpec((1, T, 1), lambda r, h: (r, 0, 0)),
            pl.BlockSpec((1, 1, T), lambda r, h: (r, 0, 0)),
        ],
        out_specs=[
            pl.BlockSpec((T, HD), lambda r, h: (r, h)),
            pl.BlockSpec((T, HD), lambda r, h: (r, h)),
            pl.BlockSpec((1, 2, T), lambda r, h: (r * heads + h, 0, 0)),
        ],
        out_shape=[half, half, jax.ShapeDtypeStruct((rows * heads, 2, T), F32)],
        scratch_shapes=[pltpu.VMEM((T, T), F32)],
        compiler_params=params(),
        cost_estimate=pl.CostEstimate(flops=rows * heads * 16 * T * T * HD, bytes_accessed=6 << 20, transcendentals=0),
        name="attend",
    )(ids, q, k, v, own_col, own_lane)


def backward_kernel(
    ids, q, k, v, dm_a, dm_b, lse, uq, uk, cos, sin, qg, kg, own_col, own_lane, dq_out, dk_out, dv_out, gq_out, gk_out, bias, low, high
):
    first = (pl.program_id(0) == 0) & (pl.program_id(1) == 0)

    @pl.when(first)
    def _():
        gq_out[...] = jnp.zeros_like(gq_out)
        gk_out[...] = jnp.zeros_like(gk_out)

    @pl.when(pl.program_id(1) == 0)
    def _():
        fill_bias(own_col, own_lane, bias)

    @pl.when(ids[2] == 0)
    def _():
        low[...] = dm_a[...].astype(F32)
        high[...] = dm_b[...].astype(F32)

    @pl.when(ids[2] == 1)
    def _():
        low[...] = dm_b[...].astype(F32)
        high[...] = dm_a[...].astype(F32)

    c, sn = cos[...], sin[...]

    def unturn(grad, u, gain):
        g = grad * c - pltpu.roll(grad, 64, 1) * sn
        r = lax.rsqrt(jnp.mean(u * u, axis=-1, keepdims=True) + norm_eps)
        n = u * r
        gain_grad = jnp.sum(g * n, axis=0, keepdims=True)
        gn = g * gain
        return r * (gn - n * jnp.mean(gn * n, axis=-1, keepdims=True)), gain_grad

    lane = lax.broadcasted_iota(jnp.int32, (T, HD), 1)
    lo_all, hi_all = low[...], high[...]
    dms = (
        jnp.where(lane < 64, lo_all, pltpu.roll(hi_all, 64, 1)).astype(BF),
        jnp.where(lane < 64, pltpu.roll(lo_all, 64, 1), hi_all).astype(BF),
    )
    dk = [None, None]
    dv = [None, None]

    def add(total, i, x):
        total[i] = x if total[i] is None else total[i] + x

    gq = jnp.zeros((1, HD), F32)
    for h in range(2):
        dq_tiles = []
        for lo, hi, keys in TILES:
            qh = q[lo:hi, h * HD : (h + 1) * HD]
            dm = dms[h][lo:hi]
            s = dot_nt(k[:keys, :], qh) * F32(SCALE * LOG2E) + bias[:keys, lo:hi]
            p = jnp.exp2(s - lse[0, h : h + 1, lo:hi])
            dp = dot_nt(v[:keys, :], dm)
            mean = jnp.sum(p * dp, axis=0, keepdims=True)
            ds = (p * (dp - mean) * F32(SCALE)).astype(BF)
            p = p.astype(BF)
            dq_tiles.append(dot_tn(k[:keys, :], ds))
            dkx = jnp.dot(ds, qh, preferred_element_type=F32)
            dvx = jnp.dot(p, dm, preferred_element_type=F32)
            for i in range(keys // HALF):
                add(dk, i, dkx[i * HALF : (i + 1) * HALF])
                add(dv, i, dvx[i * HALF : (i + 1) * HALF])
        dq = jnp.concatenate(dq_tiles, axis=1).T
        cols = slice(h * HD, (h + 1) * HD)
        du, gain_grad = unturn(dq, uq[:, cols], qg[...])
        dq_out[:, cols] = du.astype(BF)
        gq = gq + gain_grad
    du, gain_grad = unturn(jnp.concatenate(dk, axis=0), uk[...], kg[...])
    dk_out[...] = du.astype(BF)
    dv_out[...] = jnp.concatenate(dv, axis=0).astype(BF)
    gq_out[...] += gq
    gk_out[...] += gain_grad


def attend_back(ids, q, k, v, dm_a, dm_b, lse, uq, uk, cos, sin, qg, kg, own_col, own_lane):
    rows = q.shape[0] // T
    heads = k.shape[1] // HD

    def tile(cols):
        return pl.BlockSpec((T, cols), lambda r, h: (r, h))

    by_row = pl.BlockSpec((T, HD), lambda r, h: (r, 0))
    gain = pl.BlockSpec((1, HD), lambda r, h: (0, 0))
    narrow = jax.ShapeDtypeStruct((rows * T, heads * HD), BF)
    gain_shape = jax.ShapeDtypeStruct((1, HD), F32)
    return pl.pallas_call(
        backward_kernel,
        grid=(rows, heads),
        in_specs=[
            pl.BlockSpec(memory_space=pltpu.SMEM),
            tile(2 * HD),
            tile(HD),
            tile(HD),
            tile(HD),
            tile(HD),
            pl.BlockSpec((1, 2, T), lambda r, h: (r * heads + h, 0, 0)),
            tile(2 * HD),
            tile(HD),
            by_row,
            by_row,
            gain,
            gain,
            pl.BlockSpec((1, T, 1), lambda r, h: (r, 0, 0)),
            pl.BlockSpec((1, 1, T), lambda r, h: (r, 0, 0)),
        ],
        out_specs=[tile(2 * HD), tile(HD), tile(HD), gain, gain],
        out_shape=[jax.ShapeDtypeStruct((rows * T, heads * 2 * HD), BF), narrow, narrow, gain_shape, gain_shape],
        scratch_shapes=[pltpu.VMEM((T, T), F32), pltpu.VMEM((T, HD), F32), pltpu.VMEM((T, HD), F32)],
        compiler_params=params(),
        cost_estimate=pl.CostEstimate(flops=rows * heads * 40 * T * T * HD, bytes_accessed=16 << 20, transcendentals=0),
        name="attend_back",
    )(ids, q, k, v, dm_a, dm_b, lse, uq, uk, cos, sin, qg, kg, own_col, own_lane)


def pieces_kernel(lines, ids, x, w, *refs):
    n = len(refs) - 6 - (3 if lines else 0)
    ups, refs = refs[:n], refs[n:]
    if lines:
        before, gq, gk = refs[:3]
        refs = refs[3:]
    outs, gain, res = refs[:4], refs[4], refs[5]
    z, y = ids[0], ids[1]
    for i in range(4):
        block = lax.rem(z + i, 4)
        span = pl.ds(pl.multiple_of(block * 256, 256), 256)
        xb = x[:, span]
        at = 0
        dots = jnp.zeros((256, HD), F32)
        for up in ups:
            cols = slice(at, at + up.shape[1])
            got = dot_tn(xb, up[...])
            product = got * w[span, cols].astype(F32)
            for j in range(up.shape[1] // HD):
                dots = dots + product[:, j * HD : (j + 1) * HD]
            at += up.shape[1]
            got = got.astype(BF)
            if lines:
                outs[i][0:256, cols] = got
            else:
                res[:, cols] = got
        gain[0:1, span] = jnp.sum(dots.T, axis=0, keepdims=True)
        if not lines:
            for r in range(4):
                yy = lax.rem(y + r, 4)
                outs[r][pl.ds(pl.multiple_of(block * 64, 64), 64), :] = res[pl.ds(pl.multiple_of(yy * 64, 64), 64), :]
    if lines:
        row = lax.broadcasted_iota(jnp.int32, (16, D), 0)
        heads = jnp.concatenate([gq[...], gk[...], jnp.zeros((1, D - 2 * HD), F32)], axis=1)
        extra = jnp.where(row == 0, gain[0:1, :] + before[0:1, :], jnp.where(row == 1, heads, F32(0.0)))
        for out in outs:
            out[256:, :] = extra.astype(BF)


def weight_pieces(ids, x, w, ups, gains=None):
    lines = gains is not None
    gains = gains or []
    width = sum(u.shape[1] for u in ups)
    piece = jax.ShapeDtypeStruct((272 if lines else 256, width), BF)
    vm = pl.BlockSpec(memory_space=pltpu.VMEM)
    return pl.pallas_call(
        functools.partial(pieces_kernel, lines),
        in_specs=[pl.BlockSpec(memory_space=pltpu.SMEM)] + [vm] * (2 + len(ups) + len(gains)),
        out_specs=[vm] * 5,
        out_shape=[piece] * 4 + [jax.ShapeDtypeStruct((8, D), F32)],
        scratch_shapes=[pltpu.VMEM((256, width), BF)],
        compiler_params=params(),
        cost_estimate=pl.CostEstimate(flops=2 * x.shape[0] * D * width, bytes_accessed=6 << 20, transcendentals=0),
        name="weight_pieces",
    )(ids, x, w, *ups, *gains)


def add_split_kernel(which, ids, a, b, c, d, *outs):
    me = ids[which]

    def added(rows):
        total = a[rows, :].astype(F32) + b[rows, :].astype(F32) + c[rows, :].astype(F32) + d[rows, :].astype(F32)
        return total.astype(BF)

    for r in range(4):
        outs[r][0:64, :] = added(pl.ds(pl.multiple_of(lax.rem(me + r, 4) * 64, 64), 64))
        if a.shape[0] > 256:
            outs[r][64:, :] = added(slice(256, a.shape[0]))


def add_split(which, ids, parts):
    rows, width = parts[0].shape
    vm = pl.BlockSpec(memory_space=pltpu.VMEM)
    return pl.pallas_call(
        functools.partial(add_split_kernel, which),
        in_specs=[pl.BlockSpec(memory_space=pltpu.SMEM)] + [vm] * 4,
        out_specs=[vm] * 4,
        out_shape=[jax.ShapeDtypeStruct((rows - 192, width), BF)] * 4,
        compiler_params=params(),
        name="add_split",
    )(ids, *parts)


def send_pieces(pieces, axis):
    own, nxt, far, prv = pieces
    far = shift(far, axis, 2)
    return [own, shift(nxt, axis, 1), shift(prv, axis, -1), far]


def add_all(parts):
    total = parts[0].astype(F32)
    for part in parts[1:]:
        total = total + part.astype(F32)
    return total


def across_groups(x):
    return add_all([x, shift(x, "dp", 2), shift(x, "dp", 1), shift(x, "dp", -1)])


def body(tokens, cotangent, lengths, levels, level_scale, norm_gain, q_gain, k_gain, w_query, w_key, w_value, w_output):
    core, z, y = lax.axis_index("core"), lax.axis_index("z"), lax.axis_index("y")
    first = core == 0
    ids = jnp.stack([z, y, core, core]).astype(jnp.int32)

    halves = [
        jnp.concatenate([w_query[:, 1024 * i : 1024 * (i + 1)], w_key[:, 512 * i : 512 * (i + 1)], w_value[:, 512 * i : 512 * (i + 1)]], 1)
        for i in range(2)
    ]
    mine = jnp.where(first, halves[0], halves[1])
    other = swap(jnp.where(first, halves[1], halves[0]))
    block = jnp.where(first, jnp.concatenate([mine, other], 0), jnp.concatenate([other, mine], 0))
    a_parts = gather_line(gather_small(block[:, :1024], "y"), "z")
    b_parts = gather_line(gather_small(block[:, 1024:], "z"), "y")
    wo = lax.all_gather(w_output, ("z", "y"), axis=0, tiled=True)

    def pair(own):
        came = swap(own)
        return jnp.where(first, jnp.concatenate([own, came], 0), jnp.concatenate([came, own], 0))

    slots = pair(jnp.concatenate([lengths, levels], 1))
    tokens2 = pair(tokens)
    cot2 = pair(cotangent)
    owner, positions, weight = row_layout(slots[:, :4], slots[:, 4:], level_scale)
    own_col, own_lane = owner[:, :, None], owner[:, None, :]
    weight = weight.reshape(2 * T, 1)
    freqs = rope_theta ** (-jnp.arange(HD // 2, dtype=F32) * 2.0 / HD)
    angles = positions.reshape(2 * T, 1).astype(F32) * freqs[None, :]
    cos, sin = jnp.cos(angles), jnp.sin(angles)
    cos = jnp.concatenate([cos, cos], 1)
    sin = jnp.concatenate([-sin, sin], 1)

    wide = tokens2.astype(F32)
    inverse = lax.rsqrt(jnp.mean(wide * wide, axis=-1, keepdims=True) + norm_eps)
    normed = (wide * inverse * norm_gain).astype(BF)
    cotw = (cot2.astype(F32) * weight).astype(BF)
    qg, kg = q_gain[None, :], k_gain[None, :]

    q, k, v, uq, uk, wq, wkv = project(ids, normed, cos, sin, qg, kg, a_parts, b_parts)
    keep, send, lse = attend(ids, q, k, v, own_col, own_lane)
    got = swap(send)

    mixed = jnp.where(first, jnp.concatenate([keep, got], 1), jnp.concatenate([got, keep], 1))
    d_output = dot_tn(mixed, cotw).astype(BF)
    wo, d_output = lax.optimization_barrier((wo, d_output))
    d_output = lax.psum_scatter(d_output, ("z", "y"), scatter_dimension=0, tiled=True)

    def from_output(rows):
        return (dot_nt(cot2, rows) * weight).astype(BF)

    dm_send = swap(from_output(lax.dynamic_slice_in_dim(wo, 512 * (1 - core), 512, 0)))
    dm_keep = from_output(lax.dynamic_slice_in_dim(wo, 512 * core, 512, 0))
    dq, dk, dv, gq, gk = attend_back(ids, q, k, v, dm_keep, dm_send, lse, uq, uk, cos, sin, qg, kg, own_col, own_lane)

    *parts_b, gains_b = weight_pieces(ids, normed, wkv, [dk, dv])
    sum_b = send_pieces(parts_b, "y")
    *parts_a, _ = weight_pieces(ids, normed, wq, [dq], [gains_b, gq, gk])
    sum_a = send_pieces(parts_a, "z")
    sum_b = add_all(send_pieces(add_split(0, ids, sum_b), "z"))
    sum_a = add_all(send_pieces(add_split(1, ids, sum_a), "y"))
    gains = sum_a[64:68].reshape(32, HD)
    total = jnp.concatenate([sum_a[:64], sum_b], 1)
    kept = jnp.where(first, total[:32], total[32:])
    came = swap(jnp.concatenate([jnp.where(first, total[32:], total[:32]), gains], 1).astype(BF))
    gains = gains + came[:, 2048:].astype(F32)
    kept, came = kept.astype(BF), came[:, :2048]
    both = jnp.where(first, jnp.concatenate([kept, came], 1), jnp.concatenate([came, kept], 1))
    factor = 1.0 / math.sqrt(T * 128)
    both = across_groups(jnp.concatenate([both, gains.astype(BF)], 1)) * factor
    d_query = jnp.concatenate([both[:, :1024], both[:, 2048:3072]], 1)
    d_key = jnp.concatenate([both[:, 1024:1536], both[:, 3072:3584]], 1)
    d_value = jnp.concatenate([both[:, 1536:2048], both[:, 3584:4096]], 1)
    gains = both[:, 4096:].reshape(4, D)
    d_output = across_groups(d_output) * factor

    back = dot_nt(dq, wq) + dot_nt(jnp.concatenate([dk, dv], 1), wkv)
    hat = wide * inverse
    def own_row(x):
        return jnp.where(first, x[:T], x[T:])

    theirs = jnp.where(first, back[T:], back[:T]).astype(BF)
    back, hat = own_row(back) + swap(theirs).astype(F32), own_row(hat)
    scaled = back * norm_gain
    grad = own_row(inverse) * (scaled - hat * jnp.mean(scaled * hat, axis=-1, keepdims=True))
    grad_tokens = (grad + cotangent.astype(F32) * own_row(weight)).astype(BF)

    return grad_tokens, gains[0] / norm_gain, gains[1, :HD], gains[1, HD : 2 * HD], d_query, d_key, d_value, d_output


def solution(mesh):
    mesh = Mesh(mesh.devices.reshape(4, 4, 4, 2), ALL)
    shard = ("z", "y", "core")
    rows = P(ALL, None)
    weights = P(shard, None)
    return jax.shard_map(
        body,
        mesh=mesh,
        in_specs=(rows,) * 4 + (P(),) * 4 + (weights,) * 4,
        out_specs=(rows, P(), P(), P()) + (weights,) * 4,
        check_vma=False,
    )
```

```python
import functools
import math

import jax
import jax.numpy as jnp
from jax import lax
from jax.experimental import pallas as pl
from jax.experimental.pallas import tpu as pltpu
from jax.sharding import Mesh
from jax.sharding import PartitionSpec as P

norm_eps = 1e-06
rope_theta = 1000000.0
HD = 128
T = 512
D = 1024
HALF = T // 2
NEG = -1e30
LOG2E = 1.4426950408889634
SCALE = 1.0 / math.sqrt(HD)
ALL = ("dp", "z", "y", "core")
VMEM_LIMIT = 56 * 1024 * 1024
BF = jnp.bfloat16
F32 = jnp.float32


COST = pl.CostEstimate(flops=1024, bytes_accessed=1024, transcendentals=0)


def params(**kw):
    return pltpu.CompilerParams(vmem_limit_bytes=VMEM_LIMIT, **kw)


def shift(x, axis, by):
    n = lax.axis_size(axis)
    return lax.ppermute(x, axis, [(i, (i + by) % n) for i in range(n)])


def swap(x):
    return lax.ppermute(x, "core", [(0, 1), (1, 0)])


def dot_nt(a, b):
    return lax.dot_general(a, b, (((1,), (1,)), ((), ())), preferred_element_type=F32)


def dot_tn(a, b):
    return lax.dot_general(a, b, (((0,), (0,)), ((), ())), preferred_element_type=F32)


def row_layout(lengths, levels, level_scale):
    ends = jnp.cumsum(lengths, axis=1)
    starts = ends - lengths
    places = jnp.arange(T, dtype=jnp.int32)
    owner = jnp.sum((places[None, :, None] >= ends[:, None, :]).astype(jnp.int32), axis=2)
    slots = jnp.arange(lengths.shape[1], dtype=jnp.int32)
    member = owner[:, :, None] == slots[None, None, :]
    positions = places[None, :] - jnp.sum(jnp.where(member, starts[:, None, :], 0), axis=2)
    hit = levels[:, :, None] == jnp.arange(level_scale.shape[0], dtype=jnp.int32)[None, None, :]
    slot_weight = jnp.sum(jnp.where(hit, level_scale[None, None, :], F32(0.0)), axis=2)
    slot_weight = jnp.where(slots[None, :] < lengths.shape[1] - 1, slot_weight, F32(0.0))
    weight = jnp.sum(jnp.where(member, slot_weight[:, None, :], F32(0.0)), axis=2)
    return positions, weight


def cross(x, by, turned):
    pairs = []
    for z in range(4):
        for y in range(4):
            for c in range(2):
                along_z = (c == 0) != turned
                to_z, to_y = ((z + by) % 4, y) if along_z else (z, (y + by) % 4)
                pairs.append(((z * 4 + y) * 2 + c, (to_z * 4 + to_y) * 2 + c))
    return lax.ppermute(x, ("z", "y", "core"), pairs)


def gather_line(x, turned):
    far, nxt, prv = cross(x, 2, turned), cross(x, -1, turned), cross(x, 1, turned)
    return [x, nxt, far, prv]


def send_line(pieces, turned):
    own, nxt, far, prv = pieces
    far, nxt, prv = cross(far, 2, turned), cross(nxt, 1, turned), cross(prv, -1, turned)
    return [own, nxt, prv, far]


def row_of(ids, r, s):
    z, y, core = ids[0], ids[1], ids[2]
    to = lax.rem(z + r + core * (s - r), 4) * 256 + lax.rem(y + s + core * (r - s), 4) * 64
    return pl.ds(pl.multiple_of(to, 64), 64)


SMEM = pl.BlockSpec(memory_space=pltpu.SMEM)
VM = pl.BlockSpec(memory_space=pltpu.VMEM)
ANY = pl.BlockSpec(memory_space=pl.ANY)
GROUP = 4 * HD
WIDTH = 4 * GROUP
WIDE = WIDTH + HD


def simple(kernel, name, shapes, *args):
    return pl.pallas_call(
        kernel,
        in_specs=[SMEM] + [VM] * (len(args) - 1),
        out_specs=[VM] * len(shapes),
        out_shape=[jax.ShapeDtypeStruct(shape, BF) for shape in shapes],
        compiler_params=params(),
        cost_estimate=COST,
        name=name,
    )(*args)


def cut_kernel(ids, wq, wk, wv, slots, mine, send):
    for out, half in ((mine, ids[2]), (send, 1 - ids[2])):
        for h in range(4):
            at = GROUP * h
            out[0:32, at : at + 256] = wq[:, pl.ds(pl.multiple_of(half * 1024 + 256 * h, HD), 256)]
            out[0:32, at + 256 : at + 384] = wk[:, pl.ds(pl.multiple_of(half * 512 + HD * h, HD), HD)]
            out[0:32, at + 384 : at + 512] = wv[:, pl.ds(pl.multiple_of(half * 512 + HD * h, HD), HD)]
    send[32:48, :HD] = slots[...]
    send[32:48, HD:] = jnp.zeros((16, WIDTH - HD), BF)


def join_kernel(ids, mine, came, wo, block):
    at = ids[2] * 32
    block[pl.ds(pl.multiple_of(at, 32), 32), :WIDTH] = mine[...]
    block[pl.ds(pl.multiple_of(32 - at, 32), 32), :WIDTH] = came[0:32, :]
    block[:, WIDTH:] = wo[...]


def stack_kernel(ids, p0, p1, p2, p3, line, wo_line):
    for i, part in enumerate((p0, p1, p2, p3)):
        line[64 * i : 64 * i + 64, :] = part[:, :WIDTH]
        wo_line[64 * i : 64 * i + 64, :] = part[:, WIDTH:]


def lane_mean(x):
    return jnp.dot(x.astype(BF), jnp.full((HD, HD), 1.0 / HD, BF), preferred_element_type=F32)


def project_kernel(ids, normed, cos, sin, qg, kg, p0, p1, p2, p3, qkv, factors, w):
    for r, part in enumerate((p0, p1, p2, p3)):
        for s in range(4):
            w[row_of(ids, r, s), :] = part[64 * s : 64 * s + 64, :]
    chunks = [slice(HALF * i, HALF * (i + 1)) for i in range(normed.shape[0] // HALF)]
    lane = lax.broadcasted_iota(jnp.int32, (HALF, HD), 1)
    for rows in chunks:
        got = jnp.dot(normed[rows, :], w[...], preferred_element_type=F32)
        c, sn = cos[rows, :], sin[rows, :]
        kept = jnp.zeros((HALF, HD), F32)
        for i, gain in enumerate((qg, qg, kg)):
            x = got[:, HD * i : HD * (i + 1)]
            factor = lax.rsqrt(lane_mean(x * x) + norm_eps)
            high = factor.astype(BF).astype(F32)
            kept = jnp.where(lane == i, high, jnp.where(lane == i + 4, factor - high, kept))
            n = x * factor * gain[...]
            qkv[rows, HD * i : HD * (i + 1)] = (n * c + pltpu.roll(n, 64, 1) * sn).astype(BF)
        qkv[rows, 3 * HD :] = got[:, 3 * HD :].astype(BF)
        factors[rows, :] = kept.astype(BF)


def project(ids, normed, cos, sin, qg, kg, parts):
    rows = normed.shape[0]

    def whole(shape):
        return pl.BlockSpec(shape, lambda h: (0, 0))

    def by_head(rows, cols=GROUP):
        return pl.BlockSpec((rows, cols), lambda h: (0, h))

    return pl.pallas_call(
        project_kernel,
        grid=(4,),
        in_specs=[SMEM, whole((rows, D)), whole((rows, HD)), whole((rows, HD)), whole((1, HD)), whole((1, HD))] + [by_head(256)] * 4,
        out_specs=[by_head(rows), by_head(rows, HD), by_head(D)],
        out_shape=[
            jax.ShapeDtypeStruct((rows, WIDTH), BF),
            jax.ShapeDtypeStruct((rows, 4 * HD), BF),
            jax.ShapeDtypeStruct((D, WIDTH), BF),
        ],
        compiler_params=params(),
        cost_estimate=COST,
        name="project",
    )(ids, normed, cos, sin, qg, kg, *parts)


def fill_bias(start, bias):
    s = lax.broadcasted_iota(jnp.int32, (T, T), 0)
    t = lax.broadcasted_iota(jnp.int32, (T, T), 1)
    bias[...] = jnp.where((s >= start[0]) & (s <= t), F32(0.0), F32(NEG))


TILES = ((0, HALF, HALF), (HALF, T, T))
STEP = 128
PER = 2
REACH = [range(max(0, i - 2), i + 1) for i in range(T // STEP)]


def span(i):
    return slice(i * STEP, (i + 1) * STEP)


def columns(n, of):
    at = GROUP * (n // 2) + {"q": HD * (n % 2), "k": 2 * HD, "v": 3 * HD}[of]
    return slice(at, at + HD)


def forward_kernel(ids, qkv, start, keep, send, lse, bias, scores, probs):
    @pl.when((pl.program_id(0) == 0) & (pl.program_id(1) == 0))
    def _():
        probs[...] = jnp.zeros_like(probs)

    @pl.when(pl.program_id(1) == 0)
    def _():
        fill_bias(start, bias)

    def score(n):
        for lo, hi, keys in TILES:
            scores[n, :keys, lo:hi] = dot_nt(qkv[:keys, columns(n, "k")], qkv[lo:hi, columns(n, "q")])

    score(0)
    parts = []
    for n in range(2 * PER):
        if n + 1 < 2 * PER:
            score(n + 1)
        inverse = []
        for i, reach in enumerate(REACH):
            top = None
            for j in reach:
                x = scores[n, span(j), span(i)] * F32(SCALE * LOG2E) + bias[span(j), span(i)]
                scores[n, span(j), span(i)] = x
                top = x if top is None else jnp.maximum(top, x)
            top = jnp.max(top, axis=0, keepdims=True)
            total = None
            for j in reach:
                p = jnp.exp2(scores[n, span(j), span(i)] - top)
                probs[n, span(j), span(i)] = p.astype(BF)
                total = p if total is None else total + p
            total = jnp.sum(total, axis=0, keepdims=True)
            lse[n // 2, n % 2 : n % 2 + 1, span(i)] = top + jnp.log2(total)
            inverse.append(1.0 / total)
        tiles = [dot_tn(qkv[:keys, columns(n, "v")], probs[n, :keys, lo:hi]) for lo, hi, keys in TILES]
        parts.append(jnp.concatenate(tiles, axis=1) * jnp.concatenate(inverse, axis=1))
    core = ids[2]
    for m in range(PER):
        a, b = parts[2 * m : 2 * m + 2]
        low = jnp.concatenate([a[:64], b[:64]], axis=0).T.astype(BF)
        high = jnp.concatenate([a[64:], b[64:]], axis=0).T.astype(BF)
        cols = slice(HD * m, HD * (m + 1))

        @pl.when(core == 0)
        def _():
            keep[:, cols] = low
            send[:, cols] = high

        @pl.when(core == 1)
        def _():
            keep[:, cols] = high
            send[:, cols] = low


def attend(ids, qkv, start):
    rows = qkv.shape[0] // T
    heads = qkv.shape[1] // GROUP
    steps = heads // PER
    half = jax.ShapeDtypeStruct((rows * T, heads * HD), BF)
    tile = pl.BlockSpec((T, PER * HD), lambda r, h: (r, h))
    return pl.pallas_call(
        forward_kernel,
        grid=(rows, steps),
        in_specs=[SMEM, pl.BlockSpec((T, PER * GROUP), lambda r, h: (r, h)), pl.BlockSpec((1, 1, T), lambda r, h: (r, 0, 0))],
        out_specs=[tile, tile, pl.BlockSpec((PER, 2, T), lambda r, h: (r * steps + h, 0, 0))],
        out_shape=[half, half, jax.ShapeDtypeStruct((rows * heads, 2, T), F32)],
        scratch_shapes=[pltpu.VMEM((T, T), F32), pltpu.VMEM((2 * PER, T, T), F32), pltpu.VMEM((2 * PER, T, T), BF)],
        compiler_params=params(),
        cost_estimate=COST,
        name="attend",
    )(ids, qkv, start)


def backward_kernel(
    ids, qkv, dm_a, dm_b, lse, factors, cos, sin, qg, kg, start, du, gq_out, gk_out, bias, low, high, dms, scores, dprobs, probs, dscores
):
    first = (pl.program_id(0) == 0) & (pl.program_id(1) == 0)

    @pl.when(first)
    def _():
        gq_out[...] = jnp.zeros_like(gq_out)
        gk_out[...] = jnp.zeros_like(gk_out)
        probs[...] = jnp.zeros_like(probs)
        dscores[...] = jnp.zeros_like(dscores)

    @pl.when(pl.program_id(1) == 0)
    def _():
        fill_bias(start, bias)

    @pl.when(ids[2] == 0)
    def _():
        low[...] = dm_a[...].astype(F32)
        high[...] = dm_b[...].astype(F32)

    @pl.when(ids[2] == 1)
    def _():
        low[...] = dm_b[...].astype(F32)
        high[...] = dm_a[...].astype(F32)

    c, sn = cos[...], sin[...]

    def unturn(grad, turned, at, gain):
        g = grad * c - pltpu.roll(grad, 64, 1) * sn
        turned = turned.astype(F32)
        gained = turned * c - pltpu.roll(turned, 64, 1) * sn
        product = g * gained
        group = slice(HD * (at // 4), HD * (at // 4 + 1))
        lanes = lax.broadcasted_iota(jnp.int32, (HD, HD), 0) % 8
        pick = jnp.where((lanes == at % 4) | (lanes == at % 4 + 4), F32(1.0), F32(0.0)).astype(BF)
        factor = jnp.dot(factors[:, group], pick, preferred_element_type=F32)
        back = factor * (g * gain - gained * (1.0 / gain) * lane_mean(product))
        return back.astype(BF), jnp.sum(product, axis=0, keepdims=True)

    lane = lax.broadcasted_iota(jnp.int32, (T, HD), 1)
    for m in range(PER):
        lo, hi = low[:, HD * m : HD * (m + 1)], high[:, HD * m : HD * (m + 1)]
        dms[2 * m] = jnp.where(lane < 64, lo, pltpu.roll(hi, 64, 1)).astype(BF)
        dms[2 * m + 1] = jnp.where(lane < 64, pltpu.roll(lo, 64, 1), hi).astype(BF)

    def score(n):
        for lo, hi, keys in TILES:
            scores[n, :keys, lo:hi] = dot_nt(qkv[:keys, columns(n, "k")], qkv[lo:hi, columns(n, "q")])
            dprobs[n, :keys, lo:hi] = dot_nt(qkv[:keys, columns(n, "v")], dms[n, lo:hi])

    score(0)
    gq = jnp.zeros((1, HD), F32)
    gk = jnp.zeros((1, HD), F32)
    dk = dv = None
    for n in range(2 * PER):
        if n + 1 < 2 * PER:
            score(n + 1)
        for i, reach in enumerate(REACH):
            level = lse[n // 2, n % 2 : n % 2 + 1, span(i)]
            mean = None
            for j in reach:
                p = jnp.exp2(scores[n, span(j), span(i)] * F32(SCALE * LOG2E) + bias[span(j), span(i)] - level)
                scores[n, span(j), span(i)] = p
                probs[n, span(j), span(i)] = p.astype(BF)
                p = p * dprobs[n, span(j), span(i)]
                mean = p if mean is None else mean + p
            mean = jnp.sum(mean, axis=0, keepdims=True)
            for j in reach:
                ds = scores[n, span(j), span(i)] * (dprobs[n, span(j), span(i)] - mean)
                dscores[n, span(j), span(i)] = ds.astype(BF)
        if n % 2 == 0:
            dk, dv = [0.0, 0.0], [0.0, 0.0]
        q = columns(n, "q")
        dq = jnp.concatenate([dot_tn(qkv[:keys, columns(n, "k")], dscores[n, :keys, lo:hi]) for lo, hi, keys in TILES], axis=1).T
        for i in range(2):
            keys, queries = slice(i * HALF, (i + 1) * HALF), slice(i * HALF, T)
            dk[i] += jnp.dot(dscores[n, keys, queries], qkv[queries, q], preferred_element_type=F32)
            dv[i] += jnp.dot(probs[n, keys, queries], dms[n, queries], preferred_element_type=F32)
        du[:, q], more = unturn(dq * F32(SCALE), qkv[:, q], 4 * (n // 2) + n % 2, qg[...])
        gq = gq + more
        if n % 2 == 1:
            k = columns(n, "k")
            du[:, k], more = unturn(jnp.concatenate(dk, axis=0) * F32(SCALE), qkv[:, k], 4 * (n // 2) + 2, kg[...])
            gk = gk + more
            du[:, columns(n, "v")] = jnp.concatenate(dv, axis=0).astype(BF)
    gq_out[...] += gq / qg[...]
    gk_out[...] += gk / kg[...]


def attend_back(ids, qkv, dm_a, dm_b, lse, factors, cos, sin, qg, kg, start):
    rows = qkv.shape[0] // T
    heads = qkv.shape[1] // GROUP
    steps = heads // PER

    def tile(cols):
        return pl.BlockSpec((T, PER * cols), lambda r, h: (r, h))

    by_row = pl.BlockSpec((T, HD), lambda r, h: (r, 0))
    gain = pl.BlockSpec((1, HD), lambda r, h: (0, 0))
    gain_shape = jax.ShapeDtypeStruct((1, HD), F32)
    return pl.pallas_call(
        backward_kernel,
        grid=(rows, steps),
        in_specs=[
            SMEM,
            tile(GROUP),
            tile(HD),
            tile(HD),
            pl.BlockSpec((PER, 2, T), lambda r, h: (r * steps + h, 0, 0)),
            tile(HD),
            by_row,
            by_row,
            gain,
            gain,
            pl.BlockSpec((1, 1, T), lambda r, h: (r, 0, 0)),
        ],
        out_specs=[tile(GROUP), gain, gain],
        out_shape=[jax.ShapeDtypeStruct((rows * T, heads * GROUP), BF), gain_shape, gain_shape],
        scratch_shapes=[pltpu.VMEM((T, T), F32), pltpu.VMEM((T, PER * HD), F32), pltpu.VMEM((T, PER * HD), F32)]
        + [pltpu.VMEM((2 * PER, T, HD), BF)]
        + [pltpu.VMEM((2 * PER, T, T), kind) for kind in (F32, F32, BF, BF)],
        compiler_params=params(),
        cost_estimate=COST,
        name="attend_back",
    )(ids, qkv, dm_a, dm_b, lse, factors, cos, sin, qg, kg, start)


def to_mixed_kernel(ids, cot, p0, p1, p2, p3, keep, send, wo):
    @pl.when(pl.program_id(0) == 0)
    def _():
        for r, part in enumerate((p0, p1, p2, p3)):
            for s in range(4):
                wo[row_of(ids, r, s), :] = part[64 * s : 64 * s + 64, :]

    at = ids[2] * 512
    mine = wo[pl.ds(pl.multiple_of(at, 512), 512), :]
    theirs = wo[pl.ds(pl.multiple_of(512 - at, 512), 512), :]
    send[...] = dot_nt(cot[...], theirs).astype(BF)
    keep[...] = dot_nt(cot[...], mine).astype(BF)


def to_mixed(ids, cot, parts):
    rows = cot.shape[0]
    step = 512

    def by_row(cols):
        return pl.BlockSpec((step, cols), lambda i: (i, 0))

    return pl.pallas_call(
        to_mixed_kernel,
        grid=(rows // step,),
        in_specs=[SMEM, by_row(D)] + [pl.BlockSpec((256, D), lambda i: (0, 0))] * 4,
        out_specs=[by_row(512)] * 2,
        out_shape=[jax.ShapeDtypeStruct((rows, 512), BF)] * 2,
        scratch_shapes=[pltpu.VMEM((D, D), BF)],
        compiler_params=params(),
        cost_estimate=COST,
        name="to_mixed",
    )(ids, cot, *parts)


def output_pieces_kernel(ids, keep, got, cot, o0, o1, o2, o3, mixed, res):
    core = ids[2]

    @pl.when((pl.program_id(0) == 0) & (core == 0))
    def _():
        mixed[:, :512] = keep[...]
        mixed[:, 512:] = got[...]

    @pl.when((pl.program_id(0) == 0) & (core == 1))
    def _():
        mixed[:, :512] = got[...]
        mixed[:, 512:] = keep[...]

    res[...] = dot_tn(mixed[...], cot[...]).astype(BF)
    for r, out in enumerate((o0, o1, o2, o3)):
        for s in range(4):
            out[64 * s : 64 * s + 64, :] = res[row_of(ids, r, s), :]


def output_pieces(ids, keep, got, cot):
    rows = cot.shape[0]
    step = 512

    def whole(shape):
        return pl.BlockSpec(shape, lambda i: (0, 0))

    return pl.pallas_call(
        output_pieces_kernel,
        grid=(D // step,),
        in_specs=[SMEM, whole(keep.shape), whole(got.shape), pl.BlockSpec((rows, step), lambda i: (0, i))],
        out_specs=[pl.BlockSpec((256, step), lambda i: (0, i))] * 4,
        out_shape=[jax.ShapeDtypeStruct((256, D), BF)] * 4,
        scratch_shapes=[pltpu.VMEM((rows, D), BF), pltpu.VMEM((D, step), BF)],
        compiler_params=params(),
        cost_estimate=COST,
        name="output_pieces",
    )(ids, keep, got, cot)


def pieces_kernel(ids, x, w, up, gq, gk, o0, o1, o2, o3, gain, last, res, left):
    h = pl.program_id(0)
    steps = pl.num_programs(0)
    outs = (o0, o1, o2, o3)

    def departures(h):
        slot = lax.rem(h, 2)
        cols = pl.ds(pl.multiple_of(h * GROUP, GROUP), GROUP)
        return [
            pltpu.make_async_copy(res.at[slot, row_of(ids, r, s), :], out.at[64 * s : 64 * s + 64, cols], left.at[slot])
            for r, out in enumerate(outs)
            for s in range(4)
        ]

    @pl.when(h == 0)
    def _():
        gain[...] = jnp.zeros_like(gain)
        last[...] = jnp.zeros_like(last)

    @pl.when(h >= 2)
    def _():
        for copy in departures(h - 2):
            copy.wait()

    every = dot_tn(x[...], up[...])
    for i in range(4):
        block = slice(256 * i, 256 * (i + 1))
        got = every[block, :]
        res[lax.rem(h, 2), block, :] = got.astype(BF)
        product = got * w[block, :].astype(F32)
        dots = product[:, :HD]
        for j in range(1, GROUP // HD):
            dots = dots + product[:, j * HD : (j + 1) * HD]
        dots = jnp.sum(dots.T, axis=0, keepdims=True)
        gain[2 * i : 2 * i + 1, :] += dots[:, :HD]
        gain[2 * i + 1 : 2 * i + 2, :] += dots[:, HD:]
    for copy in departures(h):
        copy.start()

    @pl.when(h == steps - 1)
    def _():
        gain[8:9, :] = gq[...]
        gain[9:10, :] = gk[...]
        last[0:16, :] = gain[...].astype(BF)
        extra = [pltpu.make_async_copy(last, out.at[:, WIDTH:], left.at[2]) for out in outs]
        for copy in extra:
            copy.start()
        for copy in departures(h - 1) + departures(h) + extra:
            copy.wait()


def weight_pieces(ids, x, w, up, gq, gk):
    rows = x.shape[0]
    piece = (256, WIDTH + HD)

    def whole(shape):
        return pl.BlockSpec(shape, lambda h: (0, 0))

    def by_head(rows):
        return pl.BlockSpec((rows, GROUP), lambda h: (0, h))

    return pl.pallas_call(
        pieces_kernel,
        grid=(4,),
        in_specs=[SMEM, whole(x.shape), by_head(D), by_head(rows), whole((1, HD)), whole((1, HD))],
        out_specs=[ANY] * 4,
        out_shape=[jax.ShapeDtypeStruct(piece, BF)] * 4,
        scratch_shapes=[
            pltpu.VMEM((16, HD), F32),
            pltpu.VMEM((256, HD), BF),
            pltpu.VMEM((2, D, GROUP), BF),
            pltpu.SemaphoreType.DMA((3,)),
        ],
        compiler_params=params(),
        cost_estimate=COST,
        name="weight_pieces",
    )(ids, x, w, up, gq, gk)


def to_normed_kernel(ids, du, w, theirs, own):
    got = dot_nt(du[...], w[...])

    @pl.when(pl.program_id(0) < 2)
    def _():
        theirs[...] = got.astype(BF)

    @pl.when(pl.program_id(0) >= 2)
    def _():
        own[...] = got


def to_normed(ids, du, w):
    def block(i, ids):
        row = jnp.where(i < 2, 1 - ids[2], ids[2])
        return (2 * row + lax.rem(i, 2), 0)

    return pl.pallas_call(
        to_normed_kernel,
        grid_spec=pltpu.PrefetchScalarGridSpec(
            num_scalar_prefetch=1,
            grid=(4,),
            in_specs=[pl.BlockSpec((HALF, WIDTH), block), pl.BlockSpec((D, WIDTH), lambda i, ids: (0, 0))],
            out_specs=[
                pl.BlockSpec((HALF, D), lambda i, ids: (jnp.minimum(i, 1), 0)),
                pl.BlockSpec((HALF, D), lambda i, ids: (jnp.maximum(i - 2, 0), 0)),
            ],
        ),
        out_shape=[jax.ShapeDtypeStruct((T, D), BF), jax.ShapeDtypeStruct((T, D), F32)],
        compiler_params=params(),
        cost_estimate=COST,
        name="to_normed",
    )(ids, du, w)


def added(parts, rows, cols=slice(None)):
    total = parts[0][rows, cols].astype(F32)
    for part in parts[1:]:
        total = total + part[rows, cols].astype(F32)
    return total


def add_split_kernel(ids, *refs):
    parts, parts_o, outs = refs[:4], refs[4:8], refs[8:]
    for s, out in enumerate(outs):
        rows = slice(64 * s, 64 * s + 64)
        out[:, :WIDTH] = added(parts, rows, slice(0, WIDTH)).astype(BF)
        out[:, WIDTH:WIDE] = added(parts, slice(0, 64), slice(WIDTH, WIDE)).astype(BF)
        out[:, WIDE:] = added(parts_o, rows).astype(BF)


def share_kernel(ids, a, b, c, d, keep, send):
    parts = (a, b, c, d)
    for out, at in ((keep, ids[2] * 32), (send, 32 - ids[2] * 32)):
        out[:, :WIDTH] = added(parts, pl.ds(pl.multiple_of(at, 32), 32), slice(0, WIDTH)).astype(BF)
        out[:, WIDTH:WIDE] = added(parts, slice(0, 32), slice(WIDTH, WIDE)).astype(BF)
    for i in range(2):
        at = WIDE + D * i
        keep[:, at : at + D] = added(parts, slice(32 * i, 32 * i + 32), slice(WIDE, WIDE + D)).astype(BF)


def finish_kernel(factor, ids, gain, a, b, c, d, dq, dk, dv, do, g_norm, g_query, g_key):
    parts = (a, b, c, d)
    every = slice(None)
    second = WIDE + 2 * D
    for begin, half in ((0, ids[2]), (second, 1 - ids[2])):
        for h in range(4):
            at = begin + GROUP * h
            dq[:, pl.ds(pl.multiple_of(half * 1024 + 256 * h, HD), 256)] = added(parts, every, slice(at, at + 256)) * factor
            to = pl.ds(pl.multiple_of(half * 512 + HD * h, HD), HD)
            dk[:, to] = added(parts, every, slice(at + 256, at + 384)) * factor
            dv[:, to] = added(parts, every, slice(at + 384, at + 512)) * factor
    for i in range(2):
        at = WIDE + D * i
        do[32 * i : 32 * i + 32, :] = added(parts, every, slice(at, at + D)) * factor
    gains = [added(parts, slice(0, 16), slice(at + WIDTH, at + WIDE)) for at in (0, second)]
    gains = (gains[0] + gains[1]) * factor
    g_norm[...] = gains[0:8] / gain[...]
    g_query[...] = gains[8:9]
    g_key[...] = gains[9:10]


def finish(ids, norm_gain, parts, factor):
    shapes = [(32, 2048), (32, 1024), (32, 1024), (64, 1024), (8, HD), (1, HD), (1, HD)]
    return pl.pallas_call(
        functools.partial(finish_kernel, factor),
        in_specs=[SMEM] + [VM] * 5,
        out_specs=[VM] * 7,
        out_shape=[jax.ShapeDtypeStruct(shape, F32) for shape in shapes],
        compiler_params=params(),
        cost_estimate=COST,
        name="finish",
    )(ids, norm_gain.reshape(8, HD), *parts)


def groups_line(x):
    return [x, shift(x, "dp", 2), shift(x, "dp", 1), shift(x, "dp", -1)]


def body(tokens, cotangent, lengths, levels, level_scale, norm_gain, q_gain, k_gain, w_query, w_key, w_value, w_output):
    core, z, y = lax.axis_index("core"), lax.axis_index("z"), lax.axis_index("y")
    first = core == 0
    ids = jnp.stack([z, y, core, core]).astype(jnp.int32)

    slots = jnp.concatenate([lengths, levels], 1)
    sent = jnp.pad(slots.astype(BF), ((0, 15), (0, HD - 8)))
    mine, send = simple(cut_kernel, "cut", [(32, WIDTH), (48, WIDTH)], ids, w_query, w_key, w_value, sent)
    came = swap(send)
    (block,) = simple(join_kernel, "join", [(64, WIDTH + D)], ids, mine, came, w_output)
    line, wo_line = simple(stack_kernel, "stack", [(256, WIDTH), (256, D)], ids, *gather_line(block, True))
    parts = gather_line(line, False)

    def pair(own, other):
        return jnp.where(first, jnp.concatenate([own, other], 0), jnp.concatenate([other, own], 0))

    slots = pair(slots, came[32:33, :8].astype(jnp.int32))
    tokens2 = pair(tokens, swap(tokens))
    positions, weight = row_layout(slots[:, :4], slots[:, 4:], level_scale)
    start = (jnp.arange(T, dtype=jnp.int32)[None, :] - positions)[:, None, :]
    weight = weight.reshape(2 * T, 1)
    freqs = rope_theta ** (-jnp.arange(HD // 2, dtype=F32) * 2.0 / HD)
    angles = positions.reshape(2 * T, 1).astype(F32) * freqs[None, :]
    cos, sin = jnp.cos(angles), jnp.sin(angles)
    cos = jnp.concatenate([cos, cos], 1)
    sin = jnp.concatenate([-sin, sin], 1)

    wide = tokens2.astype(F32)
    inverse = lax.rsqrt(jnp.mean(wide * wide, axis=-1, keepdims=True) + norm_eps)
    normed = (wide * inverse * norm_gain).astype(BF)
    qg, kg = q_gain[None, :], k_gain[None, :]

    cotw = (pair(cotangent, swap(cotangent)).astype(F32) * weight).astype(BF)
    parts, wo_line, normed, cotw, start = lax.optimization_barrier((parts, wo_line, normed, cotw, start))
    wo_parts = gather_line(wo_line, False)
    qkv, factors, w = project(ids, normed, cos, sin, qg, kg, parts)
    keep, send, lse = attend(ids, qkv, start)
    got = swap(send)
    dm_keep, dm_send = to_mixed(ids, cotw, wo_parts)
    dm_got = swap(dm_send)
    sum_o = send_line(output_pieces(ids, keep, got, cotw), False)
    du, gq, gk = attend_back(ids, qkv, dm_keep, dm_got, lse, factors, cos, sin, qg, kg, start)
    du, sum_o = lax.optimization_barrier((du, sum_o))
    pieces = weight_pieces(ids, normed, w, du, gq, gk)
    pieces, du = lax.optimization_barrier((pieces, du))
    total = send_line(pieces, False)
    theirs, back = to_normed(ids, du, w)
    halves = simple(add_split_kernel, "add_split", [(64, WIDE + D)] * 4, ids, *total, *sum_o)
    kept, send = simple(share_kernel, "share", [(32, WIDE + 2 * D), (32, WIDE)], ids, *send_line(halves, True))
    both = jnp.concatenate([kept, swap(send)], 1)
    factor = 1.0 / math.sqrt(T * 128)
    d_query, d_key, d_value, d_output, g_norm, g_query, g_key = finish(ids, norm_gain, groups_line(both), factor)

    hat = wide * inverse

    def own_row(x):
        return jnp.where(first, x[:T], x[T:])

    back, hat = back + swap(theirs).astype(F32), own_row(hat)
    scaled = back * norm_gain
    grad = own_row(inverse) * (scaled - hat * jnp.mean(scaled * hat, axis=-1, keepdims=True))
    grad_tokens = (grad + cotangent.astype(F32) * own_row(weight)).astype(BF)

    return grad_tokens, g_norm.reshape(D), g_query.reshape(HD), g_key.reshape(HD), d_query, d_key, d_value, d_output


def solution(mesh):
    mesh = Mesh(mesh.devices.reshape(4, 4, 4, 2), ALL)
    shard = ("z", "y", "core")
    rows = P(ALL, None)
    weights = P(shard, None)
    return jax.shard_map(
        body,
        mesh=mesh,
        in_specs=(rows,) * 4 + (P(),) * 4 + (weights,) * 4,
        out_specs=(rows, P(), P(), P()) + (weights,) * 4,
        check_vma=False,
    )
```

```python
import functools
import math

import jax
import jax.numpy as jnp
from jax import lax
from jax.experimental import pallas as pl
from jax.experimental.pallas import tpu as pltpu
from jax.sharding import Mesh
from jax.sharding import PartitionSpec as P

norm_eps = 1e-06
rope_theta = 1000000.0
HD = 128
T = 512
D = 1024
HALF = T // 2
NEG = -1e30
LOG2E = 1.4426950408889634
SCALE = 1.0 / math.sqrt(HD)
ALL = ("dp", "z", "y", "core")
MIB = 1024 * 1024
BF = jnp.bfloat16
F32 = jnp.float32


COST = pl.CostEstimate(flops=1024, bytes_accessed=1024, transcendentals=0)


def params(mib=28):
    return pltpu.CompilerParams(vmem_limit_bytes=mib * MIB)


def shift(x, axis, by):
    n = lax.axis_size(axis)
    return lax.ppermute(x, axis, [(i, (i + by) % n) for i in range(n)])


def swap(x):
    return lax.ppermute(x, "core", [(0, 1), (1, 0)])


def dot_nt(a, b):
    return lax.dot_general(a, b, (((1,), (1,)), ((), ())), preferred_element_type=F32)


def dot_tn(a, b):
    return lax.dot_general(a, b, (((0,), (0,)), ((), ())), preferred_element_type=F32)


def row_layout(lengths, levels, level_scale):
    ends = jnp.cumsum(lengths, axis=1)
    starts = ends - lengths
    places = jnp.arange(T, dtype=jnp.int32)
    owner = jnp.sum((places[None, :, None] >= ends[:, None, :]).astype(jnp.int32), axis=2)
    slots = jnp.arange(lengths.shape[1], dtype=jnp.int32)
    member = owner[:, :, None] == slots[None, None, :]
    positions = places[None, :] - jnp.sum(jnp.where(member, starts[:, None, :], 0), axis=2)
    hit = levels[:, :, None] == jnp.arange(level_scale.shape[0], dtype=jnp.int32)[None, None, :]
    slot_weight = jnp.sum(jnp.where(hit, level_scale[None, None, :], F32(0.0)), axis=2)
    slot_weight = jnp.where(slots[None, :] < lengths.shape[1] - 1, slot_weight, F32(0.0))
    weight = jnp.sum(jnp.where(member, slot_weight[:, None, :], F32(0.0)), axis=2)
    return positions, weight


def cross(x, by, turned):
    pairs = []
    for z in range(4):
        for y in range(4):
            for c in range(2):
                along_z = (c == 0) != turned
                to_z, to_y = ((z + by) % 4, y) if along_z else (z, (y + by) % 4)
                pairs.append(((z * 4 + y) * 2 + c, (to_z * 4 + to_y) * 2 + c))
    return lax.ppermute(x, ("z", "y", "core"), pairs)


def gather_line(x, turned):
    far, nxt, prv = cross(x, 2, turned), cross(x, -1, turned), cross(x, 1, turned)
    return [x, nxt, far, prv]


def send_line(pieces, turned):
    own, nxt, far, prv = pieces
    far, nxt, prv = cross(far, 2, turned), cross(nxt, 1, turned), cross(prv, -1, turned)
    return [own, nxt, prv, far]


def row_of(ids, r, s):
    z, y, core = ids[0], ids[1], ids[2]
    to = lax.rem(z + r + core * (s - r), 4) * 256 + lax.rem(y + s + core * (r - s), 4) * 64
    return pl.ds(pl.multiple_of(to, 64), 64)


SMEM = pl.BlockSpec(memory_space=pltpu.SMEM)
VM = pl.BlockSpec(memory_space=pltpu.VMEM)
ANY = pl.BlockSpec(memory_space=pl.ANY)
GROUP = 4 * HD
WIDTH = 4 * GROUP
WIDE = WIDTH + HD


def simple(kernel, name, shapes, *args):
    return pl.pallas_call(
        kernel,
        in_specs=[SMEM] + [VM] * (len(args) - 1),
        out_specs=[VM] * len(shapes),
        out_shape=[jax.ShapeDtypeStruct(shape, BF) for shape in shapes],
        compiler_params=params(),
        cost_estimate=COST,
        name=name,
    )(*args)


def cut_kernel(ids, wq, wk, wv, slots, mine, send):
    for out, half in ((mine, ids[2]), (send, 1 - ids[2])):
        for h in range(4):
            at = GROUP * h
            out[0:32, at : at + 256] = wq[:, pl.ds(pl.multiple_of(half * 1024 + 256 * h, HD), 256)]
            out[0:32, at + 256 : at + 384] = wk[:, pl.ds(pl.multiple_of(half * 512 + HD * h, HD), HD)]
            out[0:32, at + 384 : at + 512] = wv[:, pl.ds(pl.multiple_of(half * 512 + HD * h, HD), HD)]
    send[32:48, :HD] = slots[...]
    send[32:48, HD:] = jnp.zeros((16, WIDTH - HD), BF)


def join_kernel(ids, mine, came, wo, block):
    at = ids[2] * 32
    block[pl.ds(pl.multiple_of(at, 32), 32), :WIDTH] = mine[...]
    block[pl.ds(pl.multiple_of(32 - at, 32), 32), :WIDTH] = came[0:32, :]
    block[:, WIDTH:] = wo[...]


def stack_kernel(ids, p0, p1, p2, p3, line, wo_line):
    for i, part in enumerate((p0, p1, p2, p3)):
        line[64 * i : 64 * i + 64, :] = part[:, :WIDTH]
        wo_line[64 * i : 64 * i + 64, :] = part[:, WIDTH:]


def lane_mean(x):
    return jnp.dot(x.astype(BF), jnp.full((HD, HD), 1.0 / HD, BF), preferred_element_type=F32)


def project_kernel(ids, normed, cos, sin, qg, kg, p0, p1, p2, p3, qkv, factors, w):
    for r, part in enumerate((p0, p1, p2, p3)):
        for s in range(4):
            w[row_of(ids, r, s), :] = part[64 * s : 64 * s + 64, :]
    chunks = [slice(HALF * i, HALF * (i + 1)) for i in range(normed.shape[0] // HALF)]
    lane = lax.broadcasted_iota(jnp.int32, (HALF, HD), 1)
    for rows in chunks:
        got = jnp.dot(normed[rows, :], w[...], preferred_element_type=F32)
        c, sn = cos[rows, :], sin[rows, :]
        kept = jnp.zeros((HALF, HD), F32)
        for i, gain in enumerate((qg, qg, kg)):
            x = got[:, HD * i : HD * (i + 1)]
            factor = lax.rsqrt(lane_mean(x * x) + norm_eps)
            high = factor.astype(BF).astype(F32)
            kept = jnp.where(lane == i, high, jnp.where(lane == i + 4, factor - high, kept))
            n = x * factor * gain[...]
            qkv[rows, HD * i : HD * (i + 1)] = (n * c + pltpu.roll(n, 64, 1) * sn).astype(BF)
        qkv[rows, 3 * HD :] = got[:, 3 * HD :].astype(BF)
        factors[rows, :] = kept.astype(BF)


def project(ids, normed, cos, sin, qg, kg, parts):
    rows = normed.shape[0]

    def whole(shape):
        return pl.BlockSpec(shape, lambda h: (0, 0))

    def by_head(rows, cols=GROUP):
        return pl.BlockSpec((rows, cols), lambda h: (0, h))

    return pl.pallas_call(
        project_kernel,
        grid=(4,),
        in_specs=[SMEM, whole((rows, D)), whole((rows, HD)), whole((rows, HD)), whole((1, HD)), whole((1, HD))] + [by_head(256)] * 4,
        out_specs=[by_head(rows), by_head(rows, HD), by_head(D)],
        out_shape=[
            jax.ShapeDtypeStruct((rows, WIDTH), BF),
            jax.ShapeDtypeStruct((rows, 4 * HD), BF),
            jax.ShapeDtypeStruct((D, WIDTH), BF),
        ],
        compiler_params=params(),
        cost_estimate=COST,
        name="project",
    )(ids, normed, cos, sin, qg, kg, *parts)


def fill_bias(start, bias):
    s = lax.broadcasted_iota(jnp.int32, (T, T), 0)
    t = lax.broadcasted_iota(jnp.int32, (T, T), 1)
    bias[...] = jnp.where((s >= start[0]) & (s <= t), F32(0.0), F32(NEG))


TILES = ((0, HALF, HALF), (HALF, T, T))
STEP = 128
PER = 2
REACH = [range(max(0, i - 2), i + 1) for i in range(T // STEP)]


def span(i):
    return slice(i * STEP, (i + 1) * STEP)


def columns(n, of):
    at = GROUP * (n // 2) + {"q": HD * (n % 2), "k": 2 * HD, "v": 3 * HD}[of]
    return slice(at, at + HD)


def forward_kernel(ids, qkv, start, keep, send, lse, bias, scores, probs):
    @pl.when((pl.program_id(0) == 0) & (pl.program_id(1) == 0))
    def _():
        probs[...] = jnp.zeros_like(probs)

    @pl.when(pl.program_id(1) == 0)
    def _():
        fill_bias(start, bias)

    def score(n):
        for lo, hi, keys in TILES:
            scores[n, :keys, lo:hi] = dot_nt(qkv[:keys, columns(n, "k")], qkv[lo:hi, columns(n, "q")])

    score(0)
    parts = []
    for n in range(2 * PER):
        if n + 1 < 2 * PER:
            score(n + 1)
        inverse = []
        for i, reach in enumerate(REACH):
            top = None
            for j in reach:
                x = scores[n, span(j), span(i)] * F32(SCALE * LOG2E) + bias[span(j), span(i)]
                scores[n, span(j), span(i)] = x
                top = x if top is None else jnp.maximum(top, x)
            top = jnp.max(top, axis=0, keepdims=True)
            total = None
            for j in reach:
                p = jnp.exp2(scores[n, span(j), span(i)] - top)
                probs[n, span(j), span(i)] = p.astype(BF)
                total = p if total is None else total + p
            total = jnp.sum(total, axis=0, keepdims=True)
            lse[n // 2, n % 2 : n % 2 + 1, span(i)] = top + jnp.log2(total)
            inverse.append(1.0 / total)
        tiles = [dot_tn(qkv[:keys, columns(n, "v")], probs[n, :keys, lo:hi]) for lo, hi, keys in TILES]
        parts.append(jnp.concatenate(tiles, axis=1) * jnp.concatenate(inverse, axis=1))
    core = ids[2]
    for m in range(PER):
        a, b = parts[2 * m : 2 * m + 2]
        low = jnp.concatenate([a[:64], b[:64]], axis=0).T.astype(BF)
        high = jnp.concatenate([a[64:], b[64:]], axis=0).T.astype(BF)
        cols = slice(HD * m, HD * (m + 1))

        @pl.when(core == 0)
        def _():
            keep[:, cols] = low
            send[:, cols] = high

        @pl.when(core == 1)
        def _():
            keep[:, cols] = high
            send[:, cols] = low


def attend(ids, qkv, start):
    rows = qkv.shape[0] // T
    heads = qkv.shape[1] // GROUP
    steps = heads // PER
    half = jax.ShapeDtypeStruct((rows * T, heads * HD), BF)
    tile = pl.BlockSpec((T, PER * HD), lambda r, h: (r, h))
    return pl.pallas_call(
        forward_kernel,
        grid=(rows, steps),
        in_specs=[SMEM, pl.BlockSpec((T, PER * GROUP), lambda r, h: (r, h)), pl.BlockSpec((1, 1, T), lambda r, h: (r, 0, 0))],
        out_specs=[tile, tile, pl.BlockSpec((PER, 2, T), lambda r, h: (r * steps + h, 0, 0))],
        out_shape=[half, half, jax.ShapeDtypeStruct((rows * heads, 2, T), F32)],
        scratch_shapes=[pltpu.VMEM((T, T), F32), pltpu.VMEM((2 * PER, T, T), F32), pltpu.VMEM((2 * PER, T, T), BF)],
        compiler_params=params(),
        cost_estimate=COST,
        name="attend",
    )(ids, qkv, start)


HEAD_STEPS = 4 // PER
BACK_STEPS = 2 * HEAD_STEPS


def attention_step(
    ids, qkv, dm_a, dm_b, lse, factors, cos, sin, qg, kg, start, du, gain, du_all, bias, low, high, dms, scores, dprobs, probs, dscores
):
    step = pl.program_id(0)

    @pl.when(step == 0)
    def _():
        gain[...] = jnp.zeros_like(gain)
        probs[...] = jnp.zeros_like(probs)
        dscores[...] = jnp.zeros_like(dscores)

    @pl.when(lax.rem(step, HEAD_STEPS) == 0)
    def _():
        fill_bias(start, bias)

    @pl.when(ids[2] == 0)
    def _():
        low[...] = dm_a[...].astype(F32)
        high[...] = dm_b[...].astype(F32)

    @pl.when(ids[2] == 1)
    def _():
        low[...] = dm_b[...].astype(F32)
        high[...] = dm_a[...].astype(F32)

    c, sn = cos[...], sin[...]

    def unturn(grad, turned, at, g_head):
        g = grad * c - pltpu.roll(grad, 64, 1) * sn
        turned = turned.astype(F32)
        gained = turned * c - pltpu.roll(turned, 64, 1) * sn
        product = g * gained
        group = slice(HD * (at // 4), HD * (at // 4 + 1))
        lanes = lax.broadcasted_iota(jnp.int32, (HD, HD), 0) % 8
        pick = jnp.where((lanes == at % 4) | (lanes == at % 4 + 4), F32(1.0), F32(0.0)).astype(BF)
        factor = jnp.dot(factors[:, group], pick, preferred_element_type=F32)
        back = factor * (g * g_head - gained * (1.0 / g_head) * lane_mean(product))
        return back.astype(BF), jnp.sum(product, axis=0, keepdims=True)

    lane = lax.broadcasted_iota(jnp.int32, (T, HD), 1)
    for m in range(PER):
        lo, hi = low[:, HD * m : HD * (m + 1)], high[:, HD * m : HD * (m + 1)]
        dms[2 * m] = jnp.where(lane < 64, lo, pltpu.roll(hi, 64, 1)).astype(BF)
        dms[2 * m + 1] = jnp.where(lane < 64, pltpu.roll(lo, 64, 1), hi).astype(BF)

    def score(n):
        for lo, hi, keys in TILES:
            scores[n, :keys, lo:hi] = dot_nt(qkv[:keys, columns(n, "k")], qkv[lo:hi, columns(n, "q")])
            dprobs[n, :keys, lo:hi] = dot_nt(qkv[:keys, columns(n, "v")], dms[n, lo:hi])

    score(0)
    gq = jnp.zeros((1, HD), F32)
    gk = jnp.zeros((1, HD), F32)
    dk = dv = None
    for n in range(2 * PER):
        if n + 1 < 2 * PER:
            score(n + 1)
        for i, reach in enumerate(REACH):
            level = lse[n // 2, n % 2 : n % 2 + 1, span(i)]
            mean = None
            for j in reach:
                p = jnp.exp2(scores[n, span(j), span(i)] * F32(SCALE * LOG2E) + bias[span(j), span(i)] - level)
                scores[n, span(j), span(i)] = p
                probs[n, span(j), span(i)] = p.astype(BF)
                p = p * dprobs[n, span(j), span(i)]
                mean = p if mean is None else mean + p
            mean = jnp.sum(mean, axis=0, keepdims=True)
            for j in reach:
                ds = scores[n, span(j), span(i)] * (dprobs[n, span(j), span(i)] - mean)
                dscores[n, span(j), span(i)] = ds.astype(BF)
        if n % 2 == 0:
            dk, dv = [0.0, 0.0], [0.0, 0.0]
        q = columns(n, "q")
        dq = jnp.concatenate([dot_tn(qkv[:keys, columns(n, "k")], dscores[n, :keys, lo:hi]) for lo, hi, keys in TILES], axis=1).T
        for i in range(2):
            keys, queries = slice(i * HALF, (i + 1) * HALF), slice(i * HALF, T)
            dk[i] += jnp.dot(dscores[n, keys, queries], qkv[queries, q], preferred_element_type=F32)
            dv[i] += jnp.dot(probs[n, keys, queries], dms[n, queries], preferred_element_type=F32)
        du[:, q], more = unturn(dq * F32(SCALE), qkv[:, q], 4 * (n // 2) + n % 2, qg[...])
        gq = gq + more
        if n % 2 == 1:
            k = columns(n, "k")
            du[:, k], more = unturn(jnp.concatenate(dk, axis=0) * F32(SCALE), qkv[:, k], 4 * (n // 2) + 2, kg[...])
            gk = gk + more
            du[:, columns(n, "v")] = jnp.concatenate(dv, axis=0).astype(BF)
    gain[8:9, :] += gq / qg[...]
    gain[9:10, :] += gk / kg[...]
    rows = pl.ds(pl.multiple_of(step // HEAD_STEPS * T, T), T)
    cols = pl.ds(pl.multiple_of(lax.rem(step, HEAD_STEPS) * PER * GROUP, PER * GROUP), PER * GROUP)
    du_all[rows, cols] = du[...]


def pieces_step(ids, h, outs, x, w, du_all, gain, last, res, left):
    def departures(h):
        slot = lax.rem(h, 2)
        cols = pl.ds(pl.multiple_of(h * GROUP, GROUP), GROUP)
        return [
            pltpu.make_async_copy(res.at[slot, row_of(ids, r, s), :], out.at[64 * s : 64 * s + 64, cols], left.at[slot])
            for r, out in enumerate(outs)
            for s in range(4)
        ]

    @pl.when(h >= 2)
    def _():
        for copy in departures(h - 2):
            copy.wait()

    cols = pl.ds(pl.multiple_of(h * GROUP, GROUP), GROUP)
    every = dot_tn(x[...], du_all[:, cols])
    for i in range(4):
        block = slice(256 * i, 256 * (i + 1))
        got = every[block, :]
        res[lax.rem(h, 2), block, :] = got.astype(BF)
        product = got * w[block, cols].astype(F32)
        dots = product[:, :HD]
        for j in range(1, GROUP // HD):
            dots = dots + product[:, j * HD : (j + 1) * HD]
        dots = jnp.sum(dots.T, axis=0, keepdims=True)
        gain[2 * i : 2 * i + 1, :] += dots[:, :HD]
        gain[2 * i + 1 : 2 * i + 2, :] += dots[:, HD:]
    for copy in departures(h):
        copy.start()

    @pl.when(h == 3)
    def _():
        last[...] = jnp.zeros_like(last)
        last[0:16, :] = gain[...].astype(BF)
        extra = [pltpu.make_async_copy(last, out.at[:, WIDTH:], left.at[2]) for out in outs]
        for copy in extra:
            copy.start()
        for copy in departures(h - 1) + departures(h) + extra:
            copy.wait()


def backward_kernel(
    ids, qkv, dm_a, dm_b, lse, factors, cos, sin, qg, kg, start, x_in, w_in, du, o0, o1, o2, o3, *scratch
):
    gain, last, res, left, du_all, x, w, came = scratch[:8]
    step = pl.program_id(0)
    arrivals = [pltpu.make_async_copy(x_in, x, came.at[0]), pltpu.make_async_copy(w_in, w, came.at[1])]

    @pl.when(step == 0)
    def _():
        for copy in arrivals:
            copy.start()

    @pl.when(step < BACK_STEPS)
    def _():
        attention_step(ids, qkv, dm_a, dm_b, lse, factors, cos, sin, qg, kg, start, du, gain, du_all, *scratch[8:])

    @pl.when(step == BACK_STEPS)
    def _():
        for copy in arrivals:
            copy.wait()

    @pl.when(step >= BACK_STEPS)
    def _():
        pieces_step(ids, step - BACK_STEPS, (o0, o1, o2, o3), x, w, du_all, gain, last, res, left)


def attend_back(ids, qkv, dm_a, dm_b, lse, factors, cos, sin, qg, kg, start, x, w):
    rows = qkv.shape[0]

    def at(i):
        i = jnp.minimum(i, BACK_STEPS - 1)
        return i // HEAD_STEPS, lax.rem(i, HEAD_STEPS)

    def tile(cols):
        return pl.BlockSpec((T, PER * cols), at)

    by_row = pl.BlockSpec((T, HD), lambda i: (at(i)[0], 0))
    whole = pl.BlockSpec((1, HD), lambda i: (0, 0))
    piece = jax.ShapeDtypeStruct((256, WIDE), BF)
    return pl.pallas_call(
        backward_kernel,
        grid=(BACK_STEPS + 4,),
        in_specs=[
            SMEM,
            tile(GROUP),
            tile(HD),
            tile(HD),
            pl.BlockSpec((PER, 2, T), lambda i: (jnp.minimum(i, BACK_STEPS - 1), 0, 0)),
            tile(HD),
            by_row,
            by_row,
            whole,
            whole,
            pl.BlockSpec((1, 1, T), lambda i: (at(i)[0], 0, 0)),
            ANY,
            ANY,
        ],
        out_specs=[tile(GROUP)] + [ANY] * 4,
        out_shape=[jax.ShapeDtypeStruct((rows, WIDTH), BF)] + [piece] * 4,
        scratch_shapes=[
            pltpu.VMEM((16, HD), F32),
            pltpu.VMEM((256, HD), BF),
            pltpu.VMEM((2, D, GROUP), BF),
            pltpu.SemaphoreType.DMA((3,)),
            pltpu.VMEM((rows, WIDTH), BF),
            pltpu.VMEM(x.shape, BF),
            pltpu.VMEM(w.shape, BF),
            pltpu.SemaphoreType.DMA((2,)),
            pltpu.VMEM((T, T), F32),
            pltpu.VMEM((T, PER * HD), F32),
            pltpu.VMEM((T, PER * HD), F32),
            pltpu.VMEM((2 * PER, T, HD), BF),
        ]
        + [pltpu.VMEM((2 * PER, T, T), kind) for kind in (F32, F32, BF, BF)],
        compiler_params=params(48),
        cost_estimate=COST,
        name="attend_back",
    )(ids, qkv, dm_a, dm_b, lse, factors, cos, sin, qg, kg, start, x, w)


def to_mixed_kernel(ids, cot, p0, p1, p2, p3, keep, send, wo):
    @pl.when(pl.program_id(0) == 0)
    def _():
        for r, part in enumerate((p0, p1, p2, p3)):
            for s in range(4):
                wo[row_of(ids, r, s), :] = part[64 * s : 64 * s + 64, :]

    at = ids[2] * 512
    mine = wo[pl.ds(pl.multiple_of(at, 512), 512), :]
    theirs = wo[pl.ds(pl.multiple_of(512 - at, 512), 512), :]
    send[...] = dot_nt(cot[...], theirs).astype(BF)
    keep[...] = dot_nt(cot[...], mine).astype(BF)


def to_mixed(ids, cot, parts):
    rows = cot.shape[0]
    step = 512

    def by_row(cols):
        return pl.BlockSpec((step, cols), lambda i: (i, 0))

    return pl.pallas_call(
        to_mixed_kernel,
        grid=(rows // step,),
        in_specs=[SMEM, by_row(D)] + [pl.BlockSpec((256, D), lambda i: (0, 0))] * 4,
        out_specs=[by_row(512)] * 2,
        out_shape=[jax.ShapeDtypeStruct((rows, 512), BF)] * 2,
        scratch_shapes=[pltpu.VMEM((D, D), BF)],
        compiler_params=params(),
        cost_estimate=COST,
        name="to_mixed",
    )(ids, cot, *parts)


def output_pieces_kernel(ids, keep, got, cot, o0, o1, o2, o3, mixed, res):
    core = ids[2]

    @pl.when((pl.program_id(0) == 0) & (core == 0))
    def _():
        mixed[:, :512] = keep[...]
        mixed[:, 512:] = got[...]

    @pl.when((pl.program_id(0) == 0) & (core == 1))
    def _():
        mixed[:, :512] = got[...]
        mixed[:, 512:] = keep[...]

    res[...] = dot_tn(mixed[...], cot[...]).astype(BF)
    for r, out in enumerate((o0, o1, o2, o3)):
        for s in range(4):
            out[64 * s : 64 * s + 64, :] = res[row_of(ids, r, s), :]


def output_pieces(ids, keep, got, cot):
    rows = cot.shape[0]
    step = 512

    def whole(shape):
        return pl.BlockSpec(shape, lambda i: (0, 0))

    return pl.pallas_call(
        output_pieces_kernel,
        grid=(D // step,),
        in_specs=[SMEM, whole(keep.shape), whole(got.shape), pl.BlockSpec((rows, step), lambda i: (0, i))],
        out_specs=[pl.BlockSpec((256, step), lambda i: (0, i))] * 4,
        out_shape=[jax.ShapeDtypeStruct((256, D), BF)] * 4,
        scratch_shapes=[pltpu.VMEM((rows, D), BF), pltpu.VMEM((D, step), BF)],
        compiler_params=params(),
        cost_estimate=COST,
        name="output_pieces",
    )(ids, keep, got, cot)


def to_normed_kernel(ids, du, w, theirs, own):
    got = dot_nt(du[...], w[...])

    @pl.when(pl.program_id(0) < 2)
    def _():
        theirs[...] = got.astype(BF)

    @pl.when(pl.program_id(0) >= 2)
    def _():
        own[...] = got


def to_normed(ids, du, w):
    def block(i, ids):
        row = jnp.where(i < 2, 1 - ids[2], ids[2])
        return (2 * row + lax.rem(i, 2), 0)

    return pl.pallas_call(
        to_normed_kernel,
        grid_spec=pltpu.PrefetchScalarGridSpec(
            num_scalar_prefetch=1,
            grid=(4,),
            in_specs=[pl.BlockSpec((HALF, WIDTH), block), pl.BlockSpec((D, WIDTH), lambda i, ids: (0, 0))],
            out_specs=[
                pl.BlockSpec((HALF, D), lambda i, ids: (jnp.minimum(i, 1), 0)),
                pl.BlockSpec((HALF, D), lambda i, ids: (jnp.maximum(i - 2, 0), 0)),
            ],
        ),
        out_shape=[jax.ShapeDtypeStruct((T, D), BF), jax.ShapeDtypeStruct((T, D), F32)],
        compiler_params=params(),
        cost_estimate=COST,
        name="to_normed",
    )(ids, du, w)


def added(parts, rows, cols=slice(None)):
    total = parts[0][rows, cols].astype(F32)
    for part in parts[1:]:
        total = total + part[rows, cols].astype(F32)
    return total


def add_split_kernel(ids, *refs):
    parts, parts_o, outs = refs[:4], refs[4:8], refs[8:]
    for s, out in enumerate(outs):
        rows = slice(64 * s, 64 * s + 64)
        out[:, :WIDTH] = added(parts, rows, slice(0, WIDTH)).astype(BF)
        out[:, WIDTH:WIDE] = added(parts, slice(0, 64), slice(WIDTH, WIDE)).astype(BF)
        out[:, WIDE:] = added(parts_o, rows).astype(BF)


def share_kernel(ids, a, b, c, d, keep, send):
    parts = (a, b, c, d)
    for out, at in ((keep, ids[2] * 32), (send, 32 - ids[2] * 32)):
        out[:, :WIDTH] = added(parts, pl.ds(pl.multiple_of(at, 32), 32), slice(0, WIDTH)).astype(BF)
        out[:, WIDTH:WIDE] = added(parts, slice(0, 32), slice(WIDTH, WIDE)).astype(BF)
    for i in range(2):
        at = WIDE + D * i
        keep[:, at : at + D] = added(parts, slice(32 * i, 32 * i + 32), slice(WIDE, WIDE + D)).astype(BF)


def finish_kernel(factor, ids, gain, a, b, c, d, dq, dk, dv, do, g_norm, g_query, g_key):
    parts = (a, b, c, d)
    every = slice(None)
    second = WIDE + 2 * D
    for begin, half in ((0, ids[2]), (second, 1 - ids[2])):
        for h in range(4):
            at = begin + GROUP * h
            dq[:, pl.ds(pl.multiple_of(half * 1024 + 256 * h, HD), 256)] = added(parts, every, slice(at, at + 256)) * factor
            to = pl.ds(pl.multiple_of(half * 512 + HD * h, HD), HD)
            dk[:, to] = added(parts, every, slice(at + 256, at + 384)) * factor
            dv[:, to] = added(parts, every, slice(at + 384, at + 512)) * factor
    for i in range(2):
        at = WIDE + D * i
        do[32 * i : 32 * i + 32, :] = added(parts, every, slice(at, at + D)) * factor
    gains = [added(parts, slice(0, 16), slice(at + WIDTH, at + WIDE)) for at in (0, second)]
    gains = (gains[0] + gains[1]) * factor
    g_norm[...] = gains[0:8] / gain[...]
    g_query[...] = gains[8:9]
    g_key[...] = gains[9:10]


def finish(ids, norm_gain, parts, factor):
    shapes = [(32, 2048), (32, 1024), (32, 1024), (64, 1024), (8, HD), (1, HD), (1, HD)]
    return pl.pallas_call(
        functools.partial(finish_kernel, factor),
        in_specs=[SMEM] + [VM] * 5,
        out_specs=[VM] * 7,
        out_shape=[jax.ShapeDtypeStruct(shape, F32) for shape in shapes],
        compiler_params=params(),
        cost_estimate=COST,
        name="finish",
    )(ids, norm_gain.reshape(8, HD), *parts)


def groups_line(x):
    return [x, shift(x, "dp", 2), shift(x, "dp", 1), shift(x, "dp", -1)]


def body(tokens, cotangent, lengths, levels, level_scale, norm_gain, q_gain, k_gain, w_query, w_key, w_value, w_output):
    core, z, y = lax.axis_index("core"), lax.axis_index("z"), lax.axis_index("y")
    first = core == 0
    ids = jnp.stack([z, y, core, core]).astype(jnp.int32)

    slots = jnp.concatenate([lengths, levels], 1)
    sent = jnp.pad(slots.astype(BF), ((0, 15), (0, HD - 8)))
    mine, send = simple(cut_kernel, "cut", [(32, WIDTH), (48, WIDTH)], ids, w_query, w_key, w_value, sent)
    came = swap(send)
    (block,) = simple(join_kernel, "join", [(64, WIDTH + D)], ids, mine, came, w_output)
    line, wo_line = simple(stack_kernel, "stack", [(256, WIDTH), (256, D)], ids, *gather_line(block, True))
    parts = gather_line(line, False)

    def pair(own, other):
        return jnp.where(first, jnp.concatenate([own, other], 0), jnp.concatenate([other, own], 0))

    slots = pair(slots, came[32:33, :8].astype(jnp.int32))
    tokens2 = pair(tokens, swap(tokens))
    positions, weight = row_layout(slots[:, :4], slots[:, 4:], level_scale)
    start = (jnp.arange(T, dtype=jnp.int32)[None, :] - positions)[:, None, :]
    weight = weight.reshape(2 * T, 1)
    freqs = rope_theta ** (-jnp.arange(HD // 2, dtype=F32) * 2.0 / HD)
    angles = positions.reshape(2 * T, 1).astype(F32) * freqs[None, :]
    cos, sin = jnp.cos(angles), jnp.sin(angles)
    cos = jnp.concatenate([cos, cos], 1)
    sin = jnp.concatenate([-sin, sin], 1)

    wide = tokens2.astype(F32)
    inverse = lax.rsqrt(jnp.mean(wide * wide, axis=-1, keepdims=True) + norm_eps)
    normed = (wide * inverse * norm_gain).astype(BF)
    qg, kg = q_gain[None, :], k_gain[None, :]

    cotw = (pair(cotangent, swap(cotangent)).astype(F32) * weight).astype(BF)
    parts, wo_line, normed, cotw, start = lax.optimization_barrier((parts, wo_line, normed, cotw, start))
    wo_parts = gather_line(wo_line, False)
    qkv, factors, w = project(ids, normed, cos, sin, qg, kg, parts)
    keep, send, lse = attend(ids, qkv, start)
    got = swap(send)
    dm_keep, dm_send = to_mixed(ids, cotw, wo_parts)
    dm_got = swap(dm_send)
    sum_o = send_line(output_pieces(ids, keep, got, cotw), False)
    du, *pieces = attend_back(ids, qkv, dm_keep, dm_got, lse, factors, cos, sin, qg, kg, start, normed, w)
    pieces, du, sum_o = lax.optimization_barrier((pieces, du, sum_o))
    total = send_line(pieces, False)
    theirs, back = to_normed(ids, du, w)
    halves = simple(add_split_kernel, "add_split", [(64, WIDE + D)] * 4, ids, *total, *sum_o)
    kept, send = simple(share_kernel, "share", [(32, WIDE + 2 * D), (32, WIDE)], ids, *send_line(halves, True))
    both = jnp.concatenate([kept, swap(send)], 1)
    factor = 1.0 / math.sqrt(T * 128)
    d_query, d_key, d_value, d_output, g_norm, g_query, g_key = finish(ids, norm_gain, groups_line(both), factor)

    hat = wide * inverse

    def own_row(x):
        return jnp.where(first, x[:T], x[T:])

    back, hat = back + swap(theirs).astype(F32), own_row(hat)
    scaled = back * norm_gain
    grad = own_row(inverse) * (scaled - hat * jnp.mean(scaled * hat, axis=-1, keepdims=True))
    grad_tokens = (grad + cotangent.astype(F32) * own_row(weight)).astype(BF)

    return grad_tokens, g_norm.reshape(D), g_query.reshape(HD), g_key.reshape(HD), d_query, d_key, d_value, d_output


def solution(mesh):
    mesh = Mesh(mesh.devices.reshape(4, 4, 4, 2), ALL)
    shard = ("z", "y", "core")
    rows = P(ALL, None)
    weights = P(shard, None)
    return jax.shard_map(
        body,
        mesh=mesh,
        in_specs=(rows,) * 4 + (P(),) * 4 + (weights,) * 4,
        out_specs=(rows, P(), P(), P()) + (weights,) * 4,
        check_vma=False,
    )
```

```python
import functools
import math

import jax
import jax.numpy as jnp
from jax import lax
from jax.experimental import pallas as pl
from jax.experimental.pallas import tpu as pltpu
from jax.sharding import Mesh
from jax.sharding import PartitionSpec as P

norm_eps = 1e-06
rope_theta = 1000000.0
HD = 128
T = 512
D = 1024
HALF = T // 2
NEG = -1e30
LOG2E = 1.4426950408889634
SCALE = 1.0 / math.sqrt(HD)
ALL = ("dp", "z", "y", "core")
MIB = 1024 * 1024
BF = jnp.bfloat16
F32 = jnp.float32


COST = pl.CostEstimate(flops=1024, bytes_accessed=1024, transcendentals=0)


def params(mib=28):
    return pltpu.CompilerParams(vmem_limit_bytes=mib * MIB)


def shift(x, axis, by):
    n = lax.axis_size(axis)
    return lax.ppermute(x, axis, [(i, (i + by) % n) for i in range(n)])


def swap(x):
    return lax.ppermute(x, "core", [(0, 1), (1, 0)])


def dot_nt(a, b):
    return lax.dot_general(a, b, (((1,), (1,)), ((), ())), preferred_element_type=F32)


def dot_tn(a, b):
    return lax.dot_general(a, b, (((0,), (0,)), ((), ())), preferred_element_type=F32)


def row_layout(lengths, levels, level_scale):
    ends = jnp.cumsum(lengths, axis=1)
    starts = ends - lengths
    places = jnp.arange(T, dtype=jnp.int32)
    owner = jnp.sum((places[None, :, None] >= ends[:, None, :]).astype(jnp.int32), axis=2)
    slots = jnp.arange(lengths.shape[1], dtype=jnp.int32)
    member = owner[:, :, None] == slots[None, None, :]
    positions = places[None, :] - jnp.sum(jnp.where(member, starts[:, None, :], 0), axis=2)
    hit = levels[:, :, None] == jnp.arange(level_scale.shape[0], dtype=jnp.int32)[None, None, :]
    slot_weight = jnp.sum(jnp.where(hit, level_scale[None, None, :], F32(0.0)), axis=2)
    slot_weight = jnp.where(slots[None, :] < lengths.shape[1] - 1, slot_weight, F32(0.0))
    weight = jnp.sum(jnp.where(member, slot_weight[:, None, :], F32(0.0)), axis=2)
    return positions, weight


def cross(x, by, turned):
    pairs = []
    for z in range(4):
        for y in range(4):
            for c in range(2):
                along_z = (c == 0) != turned
                to_z, to_y = ((z + by) % 4, y) if along_z else (z, (y + by) % 4)
                pairs.append(((z * 4 + y) * 2 + c, (to_z * 4 + to_y) * 2 + c))
    return lax.ppermute(x, ("z", "y", "core"), pairs)


def gather_line(x, turned):
    far, nxt, prv = cross(x, 2, turned), cross(x, -1, turned), cross(x, 1, turned)
    return [x, nxt, far, prv]


def send_line(pieces, turned):
    own, nxt, far, prv = pieces
    far, nxt, prv = cross(far, 2, turned), cross(nxt, 1, turned), cross(prv, -1, turned)
    return [own, nxt, prv, far]


def row_of(ids, r, s):
    z, y, core = ids[0], ids[1], ids[2]
    to = lax.rem(z + r + core * (s - r), 4) * 256 + lax.rem(y + s + core * (r - s), 4) * 64
    return pl.ds(pl.multiple_of(to, 64), 64)


SMEM = pl.BlockSpec(memory_space=pltpu.SMEM)
VM = pl.BlockSpec(memory_space=pltpu.VMEM)
ANY = pl.BlockSpec(memory_space=pl.ANY)
GROUP = 4 * HD
WIDTH = 4 * GROUP
WIDE = WIDTH + HD


def simple(kernel, name, shapes, *args):
    return pl.pallas_call(
        kernel,
        in_specs=[SMEM] + [VM] * (len(args) - 1),
        out_specs=[VM] * len(shapes),
        out_shape=[jax.ShapeDtypeStruct(shape, BF) for shape in shapes],
        compiler_params=params(),
        cost_estimate=COST,
        name=name,
    )(*args)


def cut_kernel(ids, wq, wk, wv, slots, mine, send):
    for out, half in ((mine, ids[2]), (send, 1 - ids[2])):
        for h in range(4):
            at = GROUP * h
            out[0:32, at : at + 256] = wq[:, pl.ds(pl.multiple_of(half * 1024 + 256 * h, HD), 256)]
            out[0:32, at + 256 : at + 384] = wk[:, pl.ds(pl.multiple_of(half * 512 + HD * h, HD), HD)]
            out[0:32, at + 384 : at + 512] = wv[:, pl.ds(pl.multiple_of(half * 512 + HD * h, HD), HD)]
    send[32:48, :HD] = slots[...]
    send[32:48, HD:] = jnp.zeros((16, WIDTH - HD), BF)


def join_kernel(ids, mine, came, wo, block):
    at = ids[2] * 32
    block[pl.ds(pl.multiple_of(at, 32), 32), :WIDTH] = mine[...]
    block[pl.ds(pl.multiple_of(32 - at, 32), 32), :WIDTH] = came[0:32, :]
    block[:, WIDTH:] = wo[...]


def stack_kernel(ids, p0, p1, p2, p3, line, wo_line):
    for i, part in enumerate((p0, p1, p2, p3)):
        line[64 * i : 64 * i + 64, :] = part[:, :WIDTH]
        wo_line[64 * i : 64 * i + 64, :] = part[:, WIDTH:]


def lane_mean(x):
    return jnp.dot(x.astype(BF), jnp.full((HD, HD), 1.0 / HD, BF), preferred_element_type=F32)


def project_kernel(ids, normed, cos, sin, qg, kg, p0, p1, p2, p3, qkv, factors, w):
    for r, part in enumerate((p0, p1, p2, p3)):
        for s in range(4):
            w[row_of(ids, r, s), :] = part[64 * s : 64 * s + 64, :]
    chunks = [slice(HALF * i, HALF * (i + 1)) for i in range(normed.shape[0] // HALF)]
    lane = lax.broadcasted_iota(jnp.int32, (HALF, HD), 1)
    for rows in chunks:
        got = jnp.dot(normed[rows, :], w[...], preferred_element_type=F32)
        c, sn = cos[rows, :], sin[rows, :]
        kept = jnp.zeros((HALF, HD), F32)
        for i, gain in enumerate((qg, qg, kg)):
            x = got[:, HD * i : HD * (i + 1)]
            factor = lax.rsqrt(lane_mean(x * x) + norm_eps)
            high = factor.astype(BF).astype(F32)
            kept = jnp.where(lane == i, high, jnp.where(lane == i + 4, factor - high, kept))
            n = x * factor * gain[...]
            qkv[rows, HD * i : HD * (i + 1)] = (n * c + pltpu.roll(n, 64, 1) * sn).astype(BF)
        qkv[rows, 3 * HD :] = got[:, 3 * HD :].astype(BF)
        factors[rows, :] = kept.astype(BF)


def project(ids, normed, cos, sin, qg, kg, parts):
    rows = normed.shape[0]

    def whole(shape):
        return pl.BlockSpec(shape, lambda h: (0, 0))

    def by_head(rows, cols=GROUP):
        return pl.BlockSpec((rows, cols), lambda h: (0, h))

    return pl.pallas_call(
        project_kernel,
        grid=(4,),
        in_specs=[SMEM, whole((rows, D)), whole((rows, HD)), whole((rows, HD)), whole((1, HD)), whole((1, HD))] + [by_head(256)] * 4,
        out_specs=[by_head(rows), by_head(rows, HD), by_head(D)],
        out_shape=[
            jax.ShapeDtypeStruct((rows, WIDTH), BF),
            jax.ShapeDtypeStruct((rows, 4 * HD), BF),
            jax.ShapeDtypeStruct((D, WIDTH), BF),
        ],
        compiler_params=params(),
        cost_estimate=COST,
        name="project",
    )(ids, normed, cos, sin, qg, kg, *parts)


def fill_bias(start, bias):
    s = lax.broadcasted_iota(jnp.int32, (T, T), 0)
    t = lax.broadcasted_iota(jnp.int32, (T, T), 1)
    bias[...] = jnp.where((s >= start[0]) & (s <= t), F32(0.0), F32(NEG))


TILES = ((0, HALF, HALF), (HALF, T, T))
STEP = 128
PER = 2
REACH = [range(max(0, i - 2), i + 1) for i in range(T // STEP)]


def span(i):
    return slice(i * STEP, (i + 1) * STEP)


def columns(n, of):
    at = GROUP * (n // 2) + {"q": HD * (n % 2), "k": 2 * HD, "v": 3 * HD}[of]
    return slice(at, at + HD)


def forward_kernel(ids, qkv, start, keep, send, lse, bias, scores, probs):
    @pl.when((pl.program_id(0) == 0) & (pl.program_id(1) == 0))
    def _():
        probs[...] = jnp.zeros_like(probs)

    @pl.when(pl.program_id(1) == 0)
    def _():
        fill_bias(start, bias)

    def score(n):
        for lo, hi, keys in TILES:
            scores[n, :keys, lo:hi] = dot_nt(qkv[:keys, columns(n, "k")], qkv[lo:hi, columns(n, "q")])

    score(0)
    parts = []
    for n in range(2 * PER):
        if n + 1 < 2 * PER:
            score(n + 1)
        inverse = []
        for i, reach in enumerate(REACH):
            top = None
            for j in reach:
                x = scores[n, span(j), span(i)] * F32(SCALE * LOG2E) + bias[span(j), span(i)]
                scores[n, span(j), span(i)] = x
                top = x if top is None else jnp.maximum(top, x)
            top = jnp.max(top, axis=0, keepdims=True)
            total = None
            for j in reach:
                p = jnp.exp2(scores[n, span(j), span(i)] - top)
                probs[n, span(j), span(i)] = p.astype(BF)
                total = p if total is None else total + p
            total = jnp.sum(total, axis=0, keepdims=True)
            lse[n // 2, n % 2 : n % 2 + 1, span(i)] = top + jnp.log2(total)
            inverse.append(1.0 / total)
        tiles = [dot_tn(qkv[:keys, columns(n, "v")], probs[n, :keys, lo:hi]) for lo, hi, keys in TILES]
        parts.append(jnp.concatenate(tiles, axis=1) * jnp.concatenate(inverse, axis=1))
    core = ids[2]
    for m in range(PER):
        a, b = parts[2 * m : 2 * m + 2]
        low = jnp.concatenate([a[:64], b[:64]], axis=0).T.astype(BF)
        high = jnp.concatenate([a[64:], b[64:]], axis=0).T.astype(BF)
        cols = slice(HD * m, HD * (m + 1))

        @pl.when(core == 0)
        def _():
            keep[:, cols] = low
            send[:, cols] = high

        @pl.when(core == 1)
        def _():
            keep[:, cols] = high
            send[:, cols] = low


def attend(ids, qkv, start):
    rows = qkv.shape[0] // T
    heads = qkv.shape[1] // GROUP
    steps = heads // PER
    half = jax.ShapeDtypeStruct((rows * T, heads * HD), BF)
    tile = pl.BlockSpec((T, PER * HD), lambda r, h: (r, h))
    return pl.pallas_call(
        forward_kernel,
        grid=(rows, steps),
        in_specs=[SMEM, pl.BlockSpec((T, PER * GROUP), lambda r, h: (r, h)), pl.BlockSpec((1, 1, T), lambda r, h: (r, 0, 0))],
        out_specs=[tile, tile, pl.BlockSpec((PER, 2, T), lambda r, h: (r * steps + h, 0, 0))],
        out_shape=[half, half, jax.ShapeDtypeStruct((rows * heads, 2, T), F32)],
        scratch_shapes=[pltpu.VMEM((T, T), F32), pltpu.VMEM((2 * PER, T, T), F32), pltpu.VMEM((2 * PER, T, T), BF)],
        compiler_params=params(),
        cost_estimate=COST,
        name="attend",
    )(ids, qkv, start)


BACK_STEPS = 2


def attention_step(
    ids, qkv, dm_a, dm_b, lse, factors, cos, sin, qg, kg, start, du, gain, du_all, bias, low, high, dms, scores, dprobs, probs, dscores
):
    step = pl.program_id(0)

    @pl.when(step == 0)
    def _():
        gain[...] = jnp.zeros_like(gain)
        probs[...] = jnp.zeros_like(probs)
        dscores[...] = jnp.zeros_like(dscores)

    fill_bias(start, bias)

    @pl.when(ids[2] == 0)
    def _():
        low[...] = dm_a[...].astype(F32)
        high[...] = dm_b[...].astype(F32)

    @pl.when(ids[2] == 1)
    def _():
        low[...] = dm_b[...].astype(F32)
        high[...] = dm_a[...].astype(F32)

    c, sn = cos[...], sin[...]

    def unturn(grad, turned, at, g_head):
        g = grad * c - pltpu.roll(grad, 64, 1) * sn
        turned = turned.astype(F32)
        gained = turned * c - pltpu.roll(turned, 64, 1) * sn
        product = g * gained
        group = slice(HD * (at // 4), HD * (at // 4 + 1))
        lanes = lax.broadcasted_iota(jnp.int32, (HD, HD), 0) % 8
        pick = jnp.where((lanes == at % 4) | (lanes == at % 4 + 4), F32(1.0), F32(0.0)).astype(BF)
        factor = jnp.dot(factors[:, group], pick, preferred_element_type=F32)
        back = factor * (g * g_head - gained * (1.0 / g_head) * lane_mean(product))
        return back.astype(BF), jnp.sum(product, axis=0, keepdims=True)

    lane = lax.broadcasted_iota(jnp.int32, (T, HD), 1)
    for m in range(PER):
        lo, hi = low[:, HD * m : HD * (m + 1)], high[:, HD * m : HD * (m + 1)]
        dms[2 * m] = jnp.where(lane < 64, lo, pltpu.roll(hi, 64, 1)).astype(BF)
        dms[2 * m + 1] = jnp.where(lane < 64, pltpu.roll(lo, 64, 1), hi).astype(BF)

    def score(n):
        for lo, hi, keys in TILES:
            scores[n, :keys, lo:hi] = dot_nt(qkv[:keys, columns(n, "k")], qkv[lo:hi, columns(n, "q")])
            dprobs[n, :keys, lo:hi] = dot_nt(qkv[:keys, columns(n, "v")], dms[n, lo:hi])

    score(0)
    gq = jnp.zeros((1, HD), F32)
    gk = jnp.zeros((1, HD), F32)
    dk = dv = None
    for n in range(2 * PER):
        if n + 1 < 2 * PER:
            score(n + 1)
        for i, reach in enumerate(REACH):
            level = lse[n // 2, n % 2 : n % 2 + 1, span(i)]
            mean = None
            for j in reach:
                p = jnp.exp2(scores[n, span(j), span(i)] * F32(SCALE * LOG2E) + bias[span(j), span(i)] - level)
                scores[n, span(j), span(i)] = p
                probs[n, span(j), span(i)] = p.astype(BF)
                p = p * dprobs[n, span(j), span(i)]
                mean = p if mean is None else mean + p
            mean = jnp.sum(mean, axis=0, keepdims=True)
            for j in reach:
                ds = scores[n, span(j), span(i)] * (dprobs[n, span(j), span(i)] - mean)
                dscores[n, span(j), span(i)] = ds.astype(BF)
        if n % 2 == 0:
            dk, dv = [0.0, 0.0], [0.0, 0.0]
        q = columns(n, "q")
        dq = jnp.concatenate([dot_tn(qkv[:keys, columns(n, "k")], dscores[n, :keys, lo:hi]) for lo, hi, keys in TILES], axis=1).T
        for i in range(2):
            keys, queries = slice(i * HALF, (i + 1) * HALF), slice(i * HALF, T)
            dk[i] += jnp.dot(dscores[n, keys, queries], qkv[queries, q], preferred_element_type=F32)
            dv[i] += jnp.dot(probs[n, keys, queries], dms[n, queries], preferred_element_type=F32)
        du[:, q], more = unturn(dq * F32(SCALE), qkv[:, q], 4 * (n // 2) + n % 2, qg[...])
        gq = gq + more
        if n % 2 == 1:
            k = columns(n, "k")
            du[:, k], more = unturn(jnp.concatenate(dk, axis=0) * F32(SCALE), qkv[:, k], 4 * (n // 2) + 2, kg[...])
            gk = gk + more
            du[:, columns(n, "v")] = jnp.concatenate(dv, axis=0).astype(BF)
    gain[8:9, :] += gq / qg[...]
    gain[9:10, :] += gk / kg[...]
    du_all[pl.ds(pl.multiple_of(step * T, T), T), :] = du[...]


def pieces_step(ids, outs, x, w, du_all, gain, last, every, res, left):
    def product(h):
        every[h % 2] = dot_tn(x[...], du_all[:, GROUP * h : GROUP * (h + 1)])

    product(0)
    sent = []
    for h in range(PER):
        if h + 1 < PER:
            product(h + 1)
        cols = slice(GROUP * h, GROUP * (h + 1))
        for i in range(4):
            block = slice(256 * i, 256 * (i + 1))
            got = every[h % 2, block, :]
            res[h, block, :] = got.astype(BF)
            times = got * w[block, cols].astype(F32)
            dots = times[:, :HD]
            for j in range(1, GROUP // HD):
                dots = dots + times[:, j * HD : (j + 1) * HD]
            dots = jnp.sum(dots.T, axis=0, keepdims=True)
            gain[2 * i : 2 * i + 1, :] += dots[:, :HD]
            gain[2 * i + 1 : 2 * i + 2, :] += dots[:, HD:]
        for r, out in enumerate(outs):
            for s in range(4):
                sent.append(pltpu.make_async_copy(res.at[h, row_of(ids, r, s), :], out.at[64 * s : 64 * s + 64, cols], left))
                sent[-1].start()
    last[...] = jnp.zeros_like(last)
    last[0:16, :] = gain[...].astype(BF)
    for out in outs:
        sent.append(pltpu.make_async_copy(last, out.at[:, PER * GROUP :], left))
        sent[-1].start()
    for copy in sent:
        copy.wait()


def backward_kernel(
    group, ids, qkv, dm_a, dm_b, lse, factors, cos, sin, qg, kg, start, x_in, w_in, du, o0, o1, o2, o3, *scratch
):
    gain, last, every, res, left, du_all, x, w, came = scratch[:9]
    step = pl.program_id(0)
    cols = slice(PER * GROUP * group, PER * GROUP * (group + 1))
    arrivals = [pltpu.make_async_copy(x_in, x, came.at[0]), pltpu.make_async_copy(w_in.at[:, cols], w, came.at[1])]

    @pl.when(step == 0)
    def _():
        for copy in arrivals:
            copy.start()

    @pl.when(step < BACK_STEPS)
    def _():
        attention_step(ids, qkv, dm_a, dm_b, lse, factors, cos, sin, qg, kg, start, du, gain, du_all, *scratch[9:])

    @pl.when(step == BACK_STEPS)
    def _():
        for copy in arrivals:
            copy.wait()
        pieces_step(ids, (o0, o1, o2, o3), x, w, du_all, gain, last, every, res, left)


def attend_back(group, ids, qkv, dm_a, dm_b, lse, factors, cos, sin, qg, kg, start, x, w):
    rows = qkv.shape[0]

    def row(i):
        return jnp.minimum(i, BACK_STEPS - 1)

    def tile(cols):
        return pl.BlockSpec((T, PER * cols), lambda i: (row(i), group))

    by_row = pl.BlockSpec((T, HD), lambda i: (row(i), 0))
    whole = pl.BlockSpec((1, HD), lambda i: (0, 0))
    width = PER * GROUP
    return pl.pallas_call(
        functools.partial(backward_kernel, group),
        grid=(BACK_STEPS + 1,),
        in_specs=[
            SMEM,
            tile(GROUP),
            tile(HD),
            tile(HD),
            pl.BlockSpec((PER, 2, T), lambda i: (4 // PER * row(i) + group, 0, 0)),
            tile(HD),
            by_row,
            by_row,
            whole,
            whole,
            pl.BlockSpec((1, 1, T), lambda i: (row(i), 0, 0)),
            ANY,
            ANY,
        ],
        out_specs=[pl.BlockSpec((T, width), lambda i: (row(i), 0))] + [ANY] * 4,
        out_shape=[jax.ShapeDtypeStruct((rows, width), BF)] + [jax.ShapeDtypeStruct((256, width + HD), BF)] * 4,
        scratch_shapes=[
            pltpu.VMEM((16, HD), F32),
            pltpu.VMEM((256, HD), BF),
            pltpu.VMEM((2, D, GROUP), F32),
            pltpu.VMEM((PER, D, GROUP), BF),
            pltpu.SemaphoreType.DMA,
            pltpu.VMEM((rows, width), BF),
            pltpu.VMEM(x.shape, BF),
            pltpu.VMEM((D, width), BF),
            pltpu.SemaphoreType.DMA((2,)),
            pltpu.VMEM((T, T), F32),
            pltpu.VMEM((T, PER * HD), F32),
            pltpu.VMEM((T, PER * HD), F32),
            pltpu.VMEM((2 * PER, T, HD), BF),
        ]
        + [pltpu.VMEM((2 * PER, T, T), kind) for kind in (F32, F32, BF, BF)],
        compiler_params=params(44),
        cost_estimate=COST,
        name="attend_back",
    )(ids, qkv, dm_a, dm_b, lse, factors, cos, sin, qg, kg, start, x, w)


def to_mixed_kernel(ids, cot, p0, p1, p2, p3, keep, send, wo):
    @pl.when(pl.program_id(0) == 0)
    def _():
        for r, part in enumerate((p0, p1, p2, p3)):
            for s in range(4):
                wo[row_of(ids, r, s), :] = part[64 * s : 64 * s + 64, :]

    at = ids[2] * 512
    mine = wo[pl.ds(pl.multiple_of(at, 512), 512), :]
    theirs = wo[pl.ds(pl.multiple_of(512 - at, 512), 512), :]
    send[...] = dot_nt(cot[...], theirs).astype(BF)
    keep[...] = dot_nt(cot[...], mine).astype(BF)


def to_mixed(ids, cot, parts):
    rows = cot.shape[0]
    step = 512

    def by_row(cols):
        return pl.BlockSpec((step, cols), lambda i: (i, 0))

    return pl.pallas_call(
        to_mixed_kernel,
        grid=(rows // step,),
        in_specs=[SMEM, by_row(D)] + [pl.BlockSpec((256, D), lambda i: (0, 0))] * 4,
        out_specs=[by_row(512)] * 2,
        out_shape=[jax.ShapeDtypeStruct((rows, 512), BF)] * 2,
        scratch_shapes=[pltpu.VMEM((D, D), BF)],
        compiler_params=params(),
        cost_estimate=COST,
        name="to_mixed",
    )(ids, cot, *parts)


def output_pieces_kernel(ids, keep, got, cot, o0, o1, o2, o3, mixed, res):
    core = ids[2]

    @pl.when((pl.program_id(0) == 0) & (core == 0))
    def _():
        mixed[:, :512] = keep[...]
        mixed[:, 512:] = got[...]

    @pl.when((pl.program_id(0) == 0) & (core == 1))
    def _():
        mixed[:, :512] = got[...]
        mixed[:, 512:] = keep[...]

    res[...] = dot_tn(mixed[...], cot[...]).astype(BF)
    for r, out in enumerate((o0, o1, o2, o3)):
        for s in range(4):
            out[64 * s : 64 * s + 64, :] = res[row_of(ids, r, s), :]


def output_pieces(ids, keep, got, cot):
    rows = cot.shape[0]
    step = 512

    def whole(shape):
        return pl.BlockSpec(shape, lambda i: (0, 0))

    return pl.pallas_call(
        output_pieces_kernel,
        grid=(D // step,),
        in_specs=[SMEM, whole(keep.shape), whole(got.shape), pl.BlockSpec((rows, step), lambda i: (0, i))],
        out_specs=[pl.BlockSpec((256, step), lambda i: (0, i))] * 4,
        out_shape=[jax.ShapeDtypeStruct((256, D), BF)] * 4,
        scratch_shapes=[pltpu.VMEM((rows, D), BF), pltpu.VMEM((D, step), BF)],
        compiler_params=params(),
        cost_estimate=COST,
        name="output_pieces",
    )(ids, keep, got, cot)


def to_normed_kernel(ids, du0, du1, w, theirs, own):
    width = PER * GROUP
    got = dot_nt(du0[...], w[:, :width]) + dot_nt(du1[...], w[:, width:])

    @pl.when(pl.program_id(0) < 2)
    def _():
        theirs[...] = got.astype(BF)

    @pl.when(pl.program_id(0) >= 2)
    def _():
        own[...] = got


def to_normed(ids, du0, du1, w):
    def block(i, ids):
        row = jnp.where(i < 2, 1 - ids[2], ids[2])
        return (2 * row + lax.rem(i, 2), 0)

    return pl.pallas_call(
        to_normed_kernel,
        grid_spec=pltpu.PrefetchScalarGridSpec(
            num_scalar_prefetch=1,
            grid=(4,),
            in_specs=[pl.BlockSpec((HALF, PER * GROUP), block)] * 2 + [pl.BlockSpec((D, WIDTH), lambda i, ids: (0, 0))],
            out_specs=[
                pl.BlockSpec((HALF, D), lambda i, ids: (jnp.minimum(i, 1), 0)),
                pl.BlockSpec((HALF, D), lambda i, ids: (jnp.maximum(i - 2, 0), 0)),
            ],
        ),
        out_shape=[jax.ShapeDtypeStruct((T, D), BF), jax.ShapeDtypeStruct((T, D), F32)],
        compiler_params=params(),
        cost_estimate=COST,
        name="to_normed",
    )(ids, du0, du1, w)


def added(parts, rows, cols=slice(None)):
    total = parts[0][rows, cols].astype(F32)
    for part in parts[1:]:
        total = total + part[rows, cols].astype(F32)
    return total


def add_split_kernel(ids, *refs):
    first, second, parts_o, outs = refs[:4], refs[4:8], refs[8:12], refs[12:]
    width = PER * GROUP
    for s, out in enumerate(outs):
        rows = slice(64 * s, 64 * s + 64)
        out[:, :width] = added(first, rows, slice(0, width)).astype(BF)
        out[:, width:WIDTH] = added(second, rows, slice(0, width)).astype(BF)
        out[:, WIDTH:WIDE] = added(first + second, slice(0, 64), slice(width, width + HD)).astype(BF)
        out[:, WIDE:] = added(parts_o, rows).astype(BF)


def share_kernel(ids, a, b, c, d, keep, send):
    parts = (a, b, c, d)
    for out, at in ((keep, ids[2] * 32), (send, 32 - ids[2] * 32)):
        out[:, :WIDTH] = added(parts, pl.ds(pl.multiple_of(at, 32), 32), slice(0, WIDTH)).astype(BF)
        out[:, WIDTH:WIDE] = added(parts, slice(0, 32), slice(WIDTH, WIDE)).astype(BF)
    for i in range(2):
        at = WIDE + D * i
        keep[:, at : at + D] = added(parts, slice(32 * i, 32 * i + 32), slice(WIDE, WIDE + D)).astype(BF)


def finish_kernel(factor, ids, gain, a, b, c, d, dq, dk, dv, do, g_norm, g_query, g_key):
    parts = (a, b, c, d)
    every = slice(None)
    second = WIDE + 2 * D
    for begin, half in ((0, ids[2]), (second, 1 - ids[2])):
        for h in range(4):
            at = begin + GROUP * h
            dq[:, pl.ds(pl.multiple_of(half * 1024 + 256 * h, HD), 256)] = added(parts, every, slice(at, at + 256)) * factor
            to = pl.ds(pl.multiple_of(half * 512 + HD * h, HD), HD)
            dk[:, to] = added(parts, every, slice(at + 256, at + 384)) * factor
            dv[:, to] = added(parts, every, slice(at + 384, at + 512)) * factor
    for i in range(2):
        at = WIDE + D * i
        do[32 * i : 32 * i + 32, :] = added(parts, every, slice(at, at + D)) * factor
    gains = [added(parts, slice(0, 16), slice(at + WIDTH, at + WIDE)) for at in (0, second)]
    gains = (gains[0] + gains[1]) * factor
    g_norm[...] = gains[0:8] / gain[...]
    g_query[...] = gains[8:9]
    g_key[...] = gains[9:10]


def finish(ids, norm_gain, parts, factor):
    shapes = [(32, 2048), (32, 1024), (32, 1024), (64, 1024), (8, HD), (1, HD), (1, HD)]
    return pl.pallas_call(
        functools.partial(finish_kernel, factor),
        in_specs=[SMEM] + [VM] * 5,
        out_specs=[VM] * 7,
        out_shape=[jax.ShapeDtypeStruct(shape, F32) for shape in shapes],
        compiler_params=params(),
        cost_estimate=COST,
        name="finish",
    )(ids, norm_gain.reshape(8, HD), *parts)


def groups_line(x):
    return [x, shift(x, "dp", 2), shift(x, "dp", 1), shift(x, "dp", -1)]


def body(tokens, cotangent, lengths, levels, level_scale, norm_gain, q_gain, k_gain, w_query, w_key, w_value, w_output):
    core, z, y = lax.axis_index("core"), lax.axis_index("z"), lax.axis_index("y")
    first = core == 0
    ids = jnp.stack([z, y, core, core]).astype(jnp.int32)

    slots = jnp.concatenate([lengths, levels], 1)
    sent = jnp.pad(slots.astype(BF), ((0, 15), (0, HD - 8)))
    mine, send = simple(cut_kernel, "cut", [(32, WIDTH), (48, WIDTH)], ids, w_query, w_key, w_value, sent)
    came = swap(send)
    (block,) = simple(join_kernel, "join", [(64, WIDTH + D)], ids, mine, came, w_output)
    line, wo_line = simple(stack_kernel, "stack", [(256, WIDTH), (256, D)], ids, *gather_line(block, True))
    parts = gather_line(line, False)

    def pair(own, other):
        return jnp.where(first, jnp.concatenate([own, other], 0), jnp.concatenate([other, own], 0))

    slots = pair(slots, came[32:33, :8].astype(jnp.int32))
    tokens2 = pair(tokens, swap(tokens))
    positions, weight = row_layout(slots[:, :4], slots[:, 4:], level_scale)
    start = (jnp.arange(T, dtype=jnp.int32)[None, :] - positions)[:, None, :]
    weight = weight.reshape(2 * T, 1)
    freqs = rope_theta ** (-jnp.arange(HD // 2, dtype=F32) * 2.0 / HD)
    angles = positions.reshape(2 * T, 1).astype(F32) * freqs[None, :]
    cos, sin = jnp.cos(angles), jnp.sin(angles)
    cos = jnp.concatenate([cos, cos], 1)
    sin = jnp.concatenate([-sin, sin], 1)

    wide = tokens2.astype(F32)
    inverse = lax.rsqrt(jnp.mean(wide * wide, axis=-1, keepdims=True) + norm_eps)
    normed = (wide * inverse * norm_gain).astype(BF)
    qg, kg = q_gain[None, :], k_gain[None, :]

    cotw = (pair(cotangent, swap(cotangent)).astype(F32) * weight).astype(BF)
    parts, wo_line, normed, cotw, start, cos, sin = lax.optimization_barrier((parts, wo_line, normed, cotw, start, cos, sin))
    wo_parts = gather_line(wo_line, False)
    qkv, factors, w = project(ids, normed, cos, sin, qg, kg, parts)
    qkv, wo_parts = lax.optimization_barrier((qkv, wo_parts))
    keep, send, lse = attend(ids, qkv, start)
    got = swap(send)
    dm_keep, dm_send = to_mixed(ids, cotw, wo_parts)
    dm_got = swap(dm_send)
    o_pieces, dm_keep = lax.optimization_barrier((output_pieces(ids, keep, got, cotw), dm_keep))
    sum_o = send_line(o_pieces, False)
    back_args = (ids, qkv, dm_keep, dm_got, lse, factors, cos, sin, qg, kg, start, normed, w)
    du0, *pieces = attend_back(0, *back_args)
    pieces, sum_o = lax.optimization_barrier((pieces, sum_o))
    first_sums = send_line(pieces, False)
    lse, du0 = lax.optimization_barrier((lse, du0))
    du1, *pieces = attend_back(1, ids, qkv, dm_keep, dm_got, lse, *back_args[5:])
    pieces, first_sums, du0, du1 = lax.optimization_barrier((pieces, first_sums, du0, du1))
    second_sums = send_line(pieces, False)
    theirs, back = to_normed(ids, du0, du1, w)
    halves = simple(add_split_kernel, "add_split", [(64, WIDE + D)] * 4, ids, *first_sums, *second_sums, *sum_o)
    kept, send = simple(share_kernel, "share", [(32, WIDE + 2 * D), (32, WIDE)], ids, *send_line(halves, True))
    both = jnp.concatenate([kept, swap(send)], 1)
    factor = 1.0 / math.sqrt(T * 128)
    d_query, d_key, d_value, d_output, g_norm, g_query, g_key = finish(ids, norm_gain, groups_line(both), factor)

    hat = wide * inverse

    def own_row(x):
        return jnp.where(first, x[:T], x[T:])

    back, hat = back + swap(theirs).astype(F32), own_row(hat)
    scaled = back * norm_gain
    grad = own_row(inverse) * (scaled - hat * jnp.mean(scaled * hat, axis=-1, keepdims=True))
    grad_tokens = (grad + cotangent.astype(F32) * own_row(weight)).astype(BF)

    return grad_tokens, g_norm.reshape(D), g_query.reshape(HD), g_key.reshape(HD), d_query, d_key, d_value, d_output


def solution(mesh):
    mesh = Mesh(mesh.devices.reshape(4, 4, 4, 2), ALL)
    shard = ("z", "y", "core")
    rows = P(ALL, None)
    weights = P(shard, None)
    return jax.shard_map(
        body,
        mesh=mesh,
        in_specs=(rows,) * 4 + (P(),) * 4 + (weights,) * 4,
        out_specs=(rows, P(), P(), P()) + (weights,) * 4,
        check_vma=False,
    )
```
